128 devices in a mesh: tm: 64 (over z, y, x), space: 2 (over core).
Axes of the slice: x: 4, y: 4, z: 4, core: 2. Of those that a mesh axis runs over, the one named last changes fastest.
Arguments:
- coeffs: float32 [4, 8, 2, 512, 1024], P(None, None, 'space', 'tm'), may hold values from -2.5 to 2.5
Outputs:
- wilson: float32 [2, 3, 3, 2, 512, 1024], P(None, None, None, 'space', 'tm')
The draws below stay inside these ranges and needn't reach their ends.
All inputs are finite; a program needn't handle non-finite values.
Results may differ from the reference program's by a relative error of at most 0.000088.
Values sent between devices are 32-bit elements; how exact they have to be, the bound alone decides.
No kernel may reach another device: no remote copies, remote signals or barrier semaphores. Data moves between devices by JAX's collectives and lax.ppermute only.
A program may use at most 64 MiB of HBM per device.

```python
import jax
import jax.numpy as jnp
from jax import lax

YDIM = 32
ZDIM = 32
NX = 2
NT = 512


def block_levels(own_key, shape, shards, low, top_value):
    def one(dim, shards_of):
        steps = jax.random.uniform(jax.random.fold_in(jax.random.fold_in(own_key, 6), dim), (shards_of,), jnp.float32, low / len(shards), top_value / len(shards))
        return jnp.repeat(jnp.exp(steps), shape[dim] // shards_of).reshape((-1,) + (1,) * (len(shape) - dim - 1))

    factor_of = one(*shards[0])
    for cut in shards[1:]:
        factor_of = factor_of * one(*cut)
    return factor_of


def noise(stream_key, shape, scale, limit, shards=(), kind=jnp.bfloat16):
    array = scale * jax.random.normal(stream_key, shape, jnp.float32)
    if shards:
        array = array * block_levels(stream_key, shape, shards, -0.22, 0.18)
    return jnp.clip(array, -limit, limit).astype(kind)


def setup_inputs(seed: int = 0) -> dict:
    key_list = jax.random.split(jax.random.key(seed), 2)
    return {
        "coeffs": noise(key_list[0], (4, 8, NX, NT, YDIM * ZDIM), 1.0, 2.5, ((2, 2), (3, 64)), jnp.float32),
    }


smear_rho = 0.1
link_degree = 8
smear_degree = 3


def cmul(left, right):
    real_part = 0.0
    imag_part = 0.0
    for middle in range(3):
        left_re = left[0][:, middle][:, None]
        left_im = left[1][:, middle][:, None]
        right_re = right[0][middle][None]
        right_im = right[1][middle][None]
        real_part = real_part + (left_re * right_re - left_im * right_im)
        imag_part = imag_part + (left_re * right_im + left_im * right_re)
    return jnp.stack([real_part, imag_part])


def dagger(matrix):
    return jnp.stack([jnp.swapaxes(matrix[0], 0, 1), -jnp.swapaxes(matrix[1], 0, 1)])


def unit_matrix(tail):
    diagonal_ones = jnp.eye(3, dtype=jnp.float32).reshape((3, 3) + (1,) * len(tail))
    real_part = jnp.broadcast_to(diagonal_ones, (3, 3) + tuple(tail))
    return jnp.stack([real_part, jnp.zeros_like(real_part)])


def taylor_exp(matrix, degree):
    identity_part = unit_matrix(matrix.shape[3:])
    result = identity_part
    for order in range(degree, 0, -1):
        result = identity_part + cmul(matrix, result) / float(order)
    return result


def algebra(coefficients):
    root_third = 1.0 / 3.0 ** 0.5
    zeroes = jnp.zeros_like(coefficients[0])
    half = [coefficients[index_a] * 0.5 for index_a in range(8)]
    herm_re = jnp.stack([
        jnp.stack([half[2] + half[7] * root_third, half[0], half[3]]),
        jnp.stack([half[0], -half[2] + half[7] * root_third, half[5]]),
        jnp.stack([half[3], half[5], -2.0 * half[7] * root_third])])
    herm_im = jnp.stack([
        jnp.stack([zeroes, -half[1], -half[4]]),
        jnp.stack([half[1], zeroes, -half[6]]),
        jnp.stack([half[4], half[6], zeroes])])
    return jnp.stack([-herm_im, herm_re])


def traceless(matrix):
    trace_sum = matrix[:, 0, 0] + matrix[:, 1, 1] + matrix[:, 2, 2]
    identity_part = unit_matrix(matrix.shape[3:])[0]
    return matrix - (trace_sum / 3.0)[:, None, None] * identity_part[None]


def neighbor(values, step_x, step_t, step_y, step_z):
    shaped = values.reshape(values.shape[:-1] + (YDIM, ZDIM))
    shaped = jnp.roll(shaped, (-step_x, -step_t, -step_y, -step_z), axis=(3, 4, 5, 6))
    return shaped.reshape(values.shape)


def reference(coeffs):
    link_field = [taylor_exp(algebra(coeffs[direction]), link_degree) for direction in range(4)]
    temporal = link_field[3]
    staple = None
    for direction in range(3):
        steps = [0, 0, 0]
        steps[direction] = 1
        spatial = link_field[direction]
        ahead_links = neighbor(spatial, 0, 1, 0, 0)
        forward = cmul(cmul(spatial, neighbor(temporal, steps[0], 0, steps[1], steps[2])), dagger(ahead_links))
        back_spatial = neighbor(spatial, -steps[0], 0, -steps[1], -steps[2])
        back_temporal = neighbor(temporal, -steps[0], 0, -steps[1], -steps[2])
        back_ahead = neighbor(ahead_links, -steps[0], 0, -steps[1], -steps[2])
        backward = cmul(cmul(dagger(back_spatial), back_temporal), back_ahead)
        staple = forward + backward if staple is None else staple + forward + backward
    force_omega = smear_rho * cmul(staple, dagger(temporal))
    antiherm = traceless((force_omega - dagger(force_omega)) * 0.5)
    smeared = cmul(taylor_exp(antiherm, smear_degree), temporal)
    sliced = jnp.moveaxis(smeared, 4, 0)

    def advance(running, link_now):
        updated = cmul(link_now, running)
        return updated, updated

    start = unit_matrix(sliced.shape[4:])
    final, products = lax.scan(advance, start, sliced, reverse=True)
    return jnp.moveaxis(products, 0, 4)
```

```python
import jax
import jax.numpy as jnp
from jax import lax
from jax.experimental import pallas as pl
from jax.experimental.pallas import tpu as pltpu
from jax.sharding import PartitionSpec as P

ZDIM = 32
LANES = 128
ROWS = 8
NT_LOCAL = 8
SMEAR = 0.1
ROOT_THIRD = 1.0 / 3.0**0.5
VMEM_LIMIT = 48 * 1024 * 1024
WHOLE = pl.BlockSpec(memory_space=pltpu.VMEM)


def read(ref, *index):
    re = [[ref[(*index, 3 * i + j)] for j in range(3)] for i in range(3)]
    im = [[ref[(*index, 9 + 3 * i + j)] for j in range(3)] for i in range(3)]
    return re, im


def write(ref, matrix, *index):
    for part in range(2):
        for i in range(3):
            for j in range(3):
                ref[(*index, 9 * part + 3 * i + j)] = matrix[part][i][j]


def dagger(matrix):
    re, im = matrix
    return (
        [[re[j][i] for j in range(3)] for i in range(3)],
        [[-im[j][i] for j in range(3)] for i in range(3)],
    )


def row_times(row, matrix, conj_left=False, conj_right=False):
    a, b = row
    c, d = matrix
    out_re, out_im = [], []
    for j in range(3):
        rr = a[0] * c[0][j]
        ii = b[0] * d[0][j]
        ri = a[0] * d[0][j]
        ir = b[0] * c[0][j]
        for m in (1, 2):
            rr = rr + a[m] * c[m][j]
            ii = ii + b[m] * d[m][j]
            ri = ri + a[m] * d[m][j]
            ir = ir + b[m] * c[m][j]
        out_re.append(rr + ii if conj_left != conj_right else rr - ii)
        if conj_left and conj_right:
            out_im.append(-(ri + ir))
        elif conj_left:
            out_im.append(ri - ir)
        elif conj_right:
            out_im.append(ir - ri)
        else:
            out_im.append(ri + ir)
    return out_re, out_im


def mul(left, right):
    re, im = [], []
    for i in range(3):
        r, m = row_times((left[0][i], left[1][i]), right)
        re.append(r)
        im.append(m)
    return re, im


def transposed(matrix):
    return tuple([[part[j][i] for j in range(3)] for i in range(3)] for part in matrix)


def forward_term(link, temporal, ahead):
    turned = transposed(ahead)
    re, im = [], []
    for i in range(3):
        row = row_times((link[0][i], link[1][i]), temporal)
        r, m = row_times(row, turned, conj_right=True)
        re.append(r)
        im.append(m)
    return re, im


def backward_term(link, temporal, ahead):
    turned = transposed(link)
    re, im = [], []
    for i in range(3):
        row = row_times((turned[0][i], turned[1][i]), temporal, conj_left=True)
        r, m = row_times(row, ahead)
        re.append(r)
        im.append(m)
    return re, im


def plus(left, right):
    return tuple(
        [[left[p][i][j] + right[p][i][j] for j in range(3)] for i in range(3)] for p in range(2)
    )


def mapped(f, matrix):
    return tuple([[f(part[i][j]) for j in range(3)] for i in range(3)] for part in matrix)


def lane():
    return lax.broadcasted_iota(jnp.int32, (ROWS, LANES), 1)


def from_y_above(x):
    r = pltpu.roll(x, LANES - ZDIM, 1)
    return jnp.where(lane() >= LANES - ZDIM, pltpu.roll(r, ROWS - 1, 0), r)


def from_y_below(x):
    r = pltpu.roll(x, ZDIM, 1)
    return jnp.where(lane() < ZDIM, pltpu.roll(r, 1, 0), r)


def from_z_above(x):
    edge = lane() % ZDIM == ZDIM - 1
    return jnp.where(edge, pltpu.roll(x, ZDIM - 1, 1), pltpu.roll(x, LANES - 1, 1))


def from_z_below(x):
    edge = lane() % ZDIM == 0
    return jnp.where(edge, pltpu.roll(x, LANES - ZDIM + 1, 1), pltpu.roll(x, 1, 1))


def squared(d, g01, g02, g12):
    n01 = g01[0] * g01[0] + g01[1] * g01[1]
    n02 = g02[0] * g02[0] + g02[1] * g02[1]
    n12 = g12[0] * g12[0] + g12[1] * g12[1]
    s = (d[0] * d[0] + (n01 + n02), d[1] * d[1] + (n01 + n12), d[2] * d[2] + (n02 + n12))
    k = (g01[0] * g12[0] - g01[1] * g12[1], g01[0] * g12[1] + g01[1] * g12[0])
    s02 = (k[0] - d[1] * g02[0], k[1] - d[1] * g02[1])
    s01 = (
        (g02[0] * g12[0] + g02[1] * g12[1]) - d[2] * g01[0],
        (g02[1] * g12[0] - g02[0] * g12[1]) - d[2] * g01[1],
    )
    s12 = (
        (g01[0] * g02[0] + g01[1] * g02[1]) - d[0] * g12[0],
        (g01[0] * g02[1] - g01[1] * g02[0]) - d[0] * g12[1],
    )
    det = (
        d[0] * (d[1] * d[2] - n12)
        - d[1] * n02
        - d[2] * n01
        + 2.0 * (k[0] * g02[0] + k[1] * g02[1])
    )
    return s, s01, s02, s12, det


def link_of(c):
    d2 = c[7] * (-2.0 * ROOT_THIRD)
    e = c[7] * ROOT_THIRD
    d = (e + c[2], e - c[2], d2)
    g01, g02, g12 = (c[0], -c[1]), (c[3], -c[4]), (c[5], -c[6])
    s, s01, s02, s12, det = squared(d, g01, g02, g12)
    p = (s[0] + s[1] + s[2]) * 0.125
    q = det * 0.125
    qq = q * q
    w = (p * (-1.0 / 5040.0) + 1.0 / 120.0) * p - 1.0 / 6.0
    f0r = qq * (p * (1.0 / 20160.0) - 1.0 / 720.0) + 1.0
    f0i = q * w
    f1r = q * ((p * (0.5 / 13440.0) - 0.5 / 360.0) * p + 0.5 / 24.0)
    f1i = (p * w + qq * (-1.0 / 5040.0)) * 0.5 + 0.5
    f2r = ((p * (0.25 / 40320.0) - 0.25 / 720.0) * p + 0.25 / 24.0) * p + (qq * (0.25 / 40320.0) - 0.125)
    f2i = q * (p * (-0.5 / 5040.0) + 0.25 / 120.0)
    re = [[None] * 3 for _ in range(3)]
    im = [[None] * 3 for _ in range(3)]
    for j in range(3):
        re[j][j] = f0r + (f1r * d[j] + f2r * s[j])
        im[j][j] = f0i + (f1i * d[j] + f2i * s[j])
    for j, k, g, h in ((0, 1, g01, s01), (0, 2, g02, s02), (1, 2, g12, s12)):
        rr = f1r * g[0] + f2r * h[0]
        ii = f1i * g[1] + f2i * h[1]
        ir = f1i * g[0] + f2i * h[0]
        ri = f1r * g[1] + f2r * h[1]
        re[j][k], re[k][j] = rr - ii, rr + ii
        im[j][k], im[k][j] = ir + ri, ir - ri
    return re, im


def smearing(staple, temporal):
    cr, ci = staple
    ur, ui = temporal

    def omega_re(j, k):
        t = cr[j][0] * ur[k][0] + ci[j][0] * ui[k][0]
        for m in (1, 2):
            t = t + (cr[j][m] * ur[k][m] + ci[j][m] * ui[k][m])
        return t

    def omega_im(j, k):
        t = ci[j][0] * ur[k][0] - cr[j][0] * ui[k][0]
        for m in (1, 2):
            t = t + (ci[j][m] * ur[k][m] - cr[j][m] * ui[k][m])
        return t

    half = 0.5 * SMEAR
    diag = [omega_im(j, j) for j in range(3)]
    third = (diag[0] + diag[1] + diag[2]) * (1.0 / 3.0)
    d = [(x - third) * SMEAR for x in diag]
    g = {}
    for j, k in ((0, 1), (0, 2), (1, 2)):
        g[j, k] = (
            (omega_im(j, k) + omega_im(k, j)) * half,
            (omega_re(k, j) - omega_re(j, k)) * half,
        )
    s, s01, s02, s12, q = squared(d, g[0, 1], g[0, 2], g[1, 2])
    p = (s[0] + s[1] + s[2]) * 0.5
    f1 = p * (-1.0 / 6.0) + 1.0
    f0i = q * (-1.0 / 6.0)
    re = [[None] * 3 for _ in range(3)]
    im = [[None] * 3 for _ in range(3)]
    for j in range(3):
        re[j][j] = 1.0 - 0.5 * s[j]
        im[j][j] = f0i + f1 * d[j]
    for j, k, h in ((0, 1, s01), (0, 2, s02), (1, 2, s12)):
        a = f1 * g[j, k][0]
        b = f1 * g[j, k][1]
        c = 0.5 * h[0]
        e = 0.5 * h[1]
        re[j][k], re[k][j] = -b - c, b - c
        im[j][k], im[k][j] = a - e, a + e
    return re, im


def slice_of(rows, direction, t):
    return [rows[direction, a, pl.ds(t, ROWS, stride=NT_LOCAL), :] for a in range(8)]


def fetch(coeffs, rows, sems, directions):
    copies = []
    for n, direction in enumerate(directions):
        for v in range(ROWS):
            copies.append(
                pltpu.make_async_copy(
                    coeffs.at[direction, :, 0, :, pl.ds(v * LANES, LANES)],
                    rows.at[n, :, pl.ds(v * NT_LOCAL, NT_LOCAL), :],
                    sems.at[n, v],
                )
            )
    return copies


def plane_terms(spatial, temporal, ahead, above, below):
    forward = forward_term(spatial, mapped(above, temporal), ahead)
    return plus(forward, mapped(below, backward_term(spatial, temporal, ahead)))


def local_kernel(coeffs, links, staple, rows, sems):
    copies = fetch(coeffs, rows, sems, range(4))
    for copy in copies:
        copy.start()
    for copy in copies:
        copy.wait()
    last = NT_LOCAL - 1
    for direction in range(4):
        write(links, link_of(slice_of(rows, direction, last)), direction, last)

    def step(i, carry):
        t = last - 1 - i
        for direction in range(4):
            write(links, link_of(slice_of(rows, direction, t)), direction, t)
        terms = plane_terms(
            read(links, 1, t), read(links, 3, t), read(links, 1, t + 1), from_y_above, from_y_below
        )
        write(staple, terms, t)
        terms = plane_terms(
            read(links, 2, t), read(links, 3, t), read(links, 2, t + 1), from_z_above, from_z_below
        )
        write(staple, plus(read(staple, t), terms), t)
        return carry

    lax.fori_loop(0, last, step, 0)


def join_kernel(
    links, staple, other, next_rows, other_next, partial, total, rows, ahead, other_ahead, other_links, terms, sems
):
    copies = fetch(other, rows, sems, (0, 3))
    for copy in copies:
        copy.start()
    last = NT_LOCAL - 1
    for direction in range(3):
        write(ahead, link_of([next_rows[direction, a] for a in range(8)]), direction)
    write(other_ahead, link_of([other_next[a] for a in range(8)]))
    write(
        terms,
        plane_terms(
            read(links, 1, last), read(links, 3, last), read(ahead, 1), from_y_above, from_y_below
        ),
    )
    write(
        terms,
        plus(
            read(terms),
            plane_terms(
                read(links, 2, last), read(links, 3, last), read(ahead, 2), from_z_above, from_z_below
            ),
        ),
    )
    one = jnp.ones((ROWS, LANES), jnp.float32)
    zero = jnp.zeros((ROWS, LANES), jnp.float32)
    unit = (
        [[one if i == j else zero for j in range(3)] for i in range(3)],
        [[zero] * 3 for _ in range(3)],
    )
    write(total, unit)
    for copy in copies:
        copy.wait()

    def step(i, carry):
        t = last - i
        write(other_links, link_of(slice_of(rows, 0, t)), 0)
        write(other_links, link_of(slice_of(rows, 1, t)), 1)
        write(
            terms,
            plus(read(terms), forward_term(read(links, 0, t), read(other_links, 1), read(ahead, 0))),
        )
        write(
            terms,
            plus(
                read(terms),
                backward_term(read(other_links, 0), read(other_links, 1), read(other_ahead)),
            ),
        )
        temporal = read(links, 3, t)
        smeared = mul(smearing(read(terms), temporal), temporal)
        running = mul(smeared, read(total))
        write(total, running)
        write(partial, running, t)
        write(ahead, read(links, 0, t), 0)
        write(other_ahead, read(other_links, 0))
        write(terms, read(staple, jnp.maximum(t - 1, 0)))
        return carry

    lax.fori_loop(0, NT_LOCAL, step, 0)


def level_kernel(low, own, by1, by2, by3, tail, new_total, new_tail, held):
    digit = lax.rem(lax.axis_index("tm") // low, 4)
    for k, ref in enumerate((own, by1, by2, by3)):
        for a in range(18):
            held[k, a] = ref[a]
    third = read(held, 3 ^ digit)
    second = mul(read(held, 2 ^ digit), third)
    first = mul(read(held, 1 ^ digit), second)
    write(new_total, mul(read(held, digit), first))
    one = jnp.ones((ROWS, LANES), jnp.float32)
    zero = jnp.zeros((ROWS, LANES), jnp.float32)
    unit = (
        [[one if i == j else zero for j in range(3)] for i in range(3)],
        [[zero] * 3 for _ in range(3)],
    )
    for k, matrix in enumerate((first, second, third, unit)):
        write(held, matrix, k)
    if tail is None:
        write(new_tail, read(held, digit))
    else:
        write(new_tail, mul(read(tail), read(held, digit)))


def first_level_kernel(low, own, by1, by2, by3, new_total, new_tail, held):
    level_kernel(low, own, by1, by2, by3, None, new_total, new_tail, held)


def closing_kernel(partial, tail, out, rows, sems):
    def step(t, carry):
        product = mul(read(partial, t), read(tail))
        for part in range(2):
            for i in range(3):
                for j in range(3):
                    rows[9 * part + 3 * i + j, pl.ds(t, ROWS, stride=NT_LOCAL), :] = product[part][i][j]
        return carry

    lax.fori_loop(0, NT_LOCAL, step, 0)
    copies = []
    for v in range(ROWS):
        copies.append(
            pltpu.make_async_copy(
                rows.at[:, pl.ds(v * NT_LOCAL, NT_LOCAL), :],
                out.at[:, :, pl.ds(v * LANES, LANES)],
                sems.at[v],
            )
        )
    for copy in copies:
        copy.start()
    for copy in copies:
        copy.wait()


def params():
    return pltpu.CompilerParams(vmem_limit_bytes=VMEM_LIMIT)


def field(*lead):
    return jax.ShapeDtypeStruct((*lead, 18, ROWS, LANES), jnp.float32)


def shards(coeffs):
    count = lax.axis_size("tm")
    next_rows = coeffs[0:3, :, 0, 0, :].reshape(3, 8, ROWS, LANES)
    other = lax.ppermute(coeffs, "space", [(0, 1), (1, 0)])
    ahead = lax.ppermute(next_rows, "tm", [((i + 1) % count, i) for i in range(count)])
    other_ahead = lax.ppermute(
        next_rows[0],
        ("tm", "space"),
        [(((i + 1) % count) * 2 + 1 - c, i * 2 + c) for i in range(count) for c in range(2)],
    )
    links, staple = pl.pallas_call(
        local_kernel,
        out_shape=(field(4, NT_LOCAL), field(NT_LOCAL)),
        in_specs=[pl.BlockSpec(memory_space=pl.ANY)],
        out_specs=(WHOLE, WHOLE),
        scratch_shapes=[
            pltpu.VMEM((4, 8, ROWS * NT_LOCAL, LANES), jnp.float32),
            pltpu.SemaphoreType.DMA((4, ROWS)),
        ],
        compiler_params=params(),
        cost_estimate=pl.CostEstimate(flops=20_000_000, bytes_accessed=4_000_000, transcendentals=0),
        name="local_terms",
    )(coeffs)
    partial, total = pl.pallas_call(
        join_kernel,
        out_shape=(field(NT_LOCAL), field()),
        in_specs=[WHOLE, WHOLE, pl.BlockSpec(memory_space=pl.ANY), WHOLE, WHOLE],
        out_specs=(WHOLE, WHOLE),
        scratch_shapes=[
            pltpu.VMEM((2, 8, ROWS * NT_LOCAL, LANES), jnp.float32),
            pltpu.VMEM((3, 18, ROWS, LANES), jnp.float32),
            pltpu.VMEM((18, ROWS, LANES), jnp.float32),
            pltpu.VMEM((2, 18, ROWS, LANES), jnp.float32),
            pltpu.VMEM((18, ROWS, LANES), jnp.float32),
            pltpu.SemaphoreType.DMA((2, ROWS)),
        ],
        compiler_params=params(),
        name="smear_and_join",
    )(links, staple, other, ahead, other_ahead)
    tail = None
    low = 1
    while low < count:
        received = [
            lax.ppermute(total, "tm", [(i, i ^ (low * k)) for i in range(count)]) for k in (1, 2, 3)
        ]
        kernel = first_level_kernel if tail is None else level_kernel
        operands = [total, *received] + ([] if tail is None else [tail])

        def body(*refs, kernel=kernel, low=low):
            kernel(low, *refs)

        total, tail = pl.pallas_call(
            body,
            out_shape=(field(), field()),
            in_specs=[WHOLE] * len(operands),
            out_specs=(WHOLE, WHOLE),
            scratch_shapes=[pltpu.VMEM((4, 18, ROWS, LANES), jnp.float32)],
            compiler_params=params(),
            name=f"level_{low}",
        )(*operands)
        low *= 4
    out = pl.pallas_call(
        closing_kernel,
        out_shape=jax.ShapeDtypeStruct((18, NT_LOCAL, ROWS * LANES), jnp.float32),
        in_specs=[WHOLE, WHOLE],
        out_specs=pl.BlockSpec(memory_space=pl.ANY),
        scratch_shapes=[
            pltpu.VMEM((18, ROWS * NT_LOCAL, LANES), jnp.float32),
            pltpu.SemaphoreType.DMA((ROWS,)),
        ],
        compiler_params=params(),
        name="closing",
    )(partial, tail)
    return out.reshape(2, 3, 3, 1, NT_LOCAL, ROWS * LANES)


def solution(mesh):
    in_specs = (P(None, None, "space", "tm", None),)
    out_specs = P(None, None, None, "space", "tm", None)
    return jax.shard_map(shards, mesh=mesh, in_specs=in_specs, out_specs=out_specs, check_vma=False)
```

```python
import jax
import jax.numpy as jnp
from jax import lax
from jax.experimental import pallas as pl
from jax.experimental.pallas import tpu as pltpu
from jax.sharding import PartitionSpec as P

ZDIM = 32
LANES = 128
ROWS = 8
NT_LOCAL = 8
SMEAR = 0.1
SPLIT = 2
PEERS = (1, 3, 2)
LAST_PEERS = (1, 3, 2)
ROOT_THIRD = 1.0 / 3.0**0.5
VMEM_LIMIT = 48 * 1024 * 1024
WHOLE = pl.BlockSpec(memory_space=pltpu.VMEM)


def read(ref, *index):
    re = [[ref[(*index, 3 * i + j)] for j in range(3)] for i in range(3)]
    im = [[ref[(*index, 9 + 3 * i + j)] for j in range(3)] for i in range(3)]
    return re, im


def write(ref, matrix, *index):
    for part in range(2):
        for i in range(3):
            for j in range(3):
                ref[(*index, 9 * part + 3 * i + j)] = matrix[part][i][j]


def row_times(row, matrix, conj_left=False, conj_right=False):
    a, b = row
    c, d = matrix
    out_re, out_im = [], []
    for j in range(3):
        rr = a[0] * c[0][j]
        ii = b[0] * d[0][j]
        ri = a[0] * d[0][j]
        ir = b[0] * c[0][j]
        for m in (1, 2):
            rr = rr + a[m] * c[m][j]
            ii = ii + b[m] * d[m][j]
            ri = ri + a[m] * d[m][j]
            ir = ir + b[m] * c[m][j]
        out_re.append(rr + ii if conj_left != conj_right else rr - ii)
        if conj_left and conj_right:
            out_im.append(-(ri + ir))
        elif conj_left:
            out_im.append(ri - ir)
        elif conj_right:
            out_im.append(ir - ri)
        else:
            out_im.append(ri + ir)
    return out_re, out_im


def mul(left, right):
    re, im = [], []
    for i in range(3):
        r, m = row_times((left[0][i], left[1][i]), right)
        re.append(r)
        im.append(m)
    return re, im


def transposed(matrix):
    return tuple([[part[j][i] for j in range(3)] for i in range(3)] for part in matrix)


def forward_term(link, temporal, ahead):
    turned = transposed(ahead)
    re, im = [], []
    for i in range(3):
        row = row_times((link[0][i], link[1][i]), temporal)
        r, m = row_times(row, turned, conj_right=True)
        re.append(r)
        im.append(m)
    return re, im


def backward_term(link, temporal, ahead):
    turned = transposed(link)
    re, im = [], []
    for i in range(3):
        row = row_times((turned[0][i], turned[1][i]), temporal, conj_left=True)
        r, m = row_times(row, ahead)
        re.append(r)
        im.append(m)
    return re, im


def plus(left, right):
    return tuple(
        [[left[p][i][j] + right[p][i][j] for j in range(3)] for i in range(3)] for p in range(2)
    )


def mapped(f, matrix):
    return tuple([[f(part[i][j]) for j in range(3)] for i in range(3)] for part in matrix)


def lane():
    return lax.broadcasted_iota(jnp.int32, (ROWS, LANES), 1)


def from_y_above(x):
    r = pltpu.roll(x, LANES - ZDIM, 1)
    return jnp.where(lane() >= LANES - ZDIM, pltpu.roll(r, ROWS - 1, 0), r)


def from_y_below(x):
    r = pltpu.roll(x, ZDIM, 1)
    return jnp.where(lane() < ZDIM, pltpu.roll(r, 1, 0), r)


def from_z_above(x):
    edge = lane() % ZDIM == ZDIM - 1
    return jnp.where(edge, pltpu.roll(x, ZDIM - 1, 1), pltpu.roll(x, LANES - 1, 1))


def from_z_below(x):
    edge = lane() % ZDIM == 0
    return jnp.where(edge, pltpu.roll(x, LANES - ZDIM + 1, 1), pltpu.roll(x, 1, 1))


def squared(d, g01, g02, g12):
    n01 = g01[0] * g01[0] + g01[1] * g01[1]
    n02 = g02[0] * g02[0] + g02[1] * g02[1]
    n12 = g12[0] * g12[0] + g12[1] * g12[1]
    s = (d[0] * d[0] + (n01 + n02), d[1] * d[1] + (n01 + n12), d[2] * d[2] + (n02 + n12))
    k = (g01[0] * g12[0] - g01[1] * g12[1], g01[0] * g12[1] + g01[1] * g12[0])
    s02 = (k[0] - d[1] * g02[0], k[1] - d[1] * g02[1])
    s01 = (
        (g02[0] * g12[0] + g02[1] * g12[1]) - d[2] * g01[0],
        (g02[1] * g12[0] - g02[0] * g12[1]) - d[2] * g01[1],
    )
    s12 = (
        (g01[0] * g02[0] + g01[1] * g02[1]) - d[0] * g12[0],
        (g01[0] * g02[1] - g01[1] * g02[0]) - d[0] * g12[1],
    )
    det = (
        d[0] * (d[1] * d[2] - n12)
        - d[1] * n02
        - d[2] * n01
        + 2.0 * (k[0] * g02[0] + k[1] * g02[1])
    )
    return s, s01, s02, s12, det


def link_of(c):
    d2 = c[7] * (-2.0 * ROOT_THIRD)
    e = c[7] * ROOT_THIRD
    d = (e + c[2], e - c[2], d2)
    g01, g02, g12 = (c[0], -c[1]), (c[3], -c[4]), (c[5], -c[6])
    s, s01, s02, s12, det = squared(d, g01, g02, g12)
    p = (s[0] + s[1] + s[2]) * 0.125
    q = det * 0.125
    qq = q * q
    w = (p * (-1.0 / 5040.0) + 1.0 / 120.0) * p - 1.0 / 6.0
    f0r = qq * (p * (1.0 / 20160.0) - 1.0 / 720.0) + 1.0
    f0i = q * w
    f1r = q * ((p * (0.5 / 13440.0) - 0.5 / 360.0) * p + 0.5 / 24.0)
    f1i = (p * w + qq * (-1.0 / 5040.0)) * 0.5 + 0.5
    f2r = ((p * (0.25 / 40320.0) - 0.25 / 720.0) * p + 0.25 / 24.0) * p + (qq * (0.25 / 40320.0) - 0.125)
    f2i = q * (p * (-0.5 / 5040.0) + 0.25 / 120.0)
    re = [[None] * 3 for _ in range(3)]
    im = [[None] * 3 for _ in range(3)]
    for j in range(3):
        re[j][j] = f0r + (f1r * d[j] + f2r * s[j])
        im[j][j] = f0i + (f1i * d[j] + f2i * s[j])
    for j, k, g, h in ((0, 1, g01, s01), (0, 2, g02, s02), (1, 2, g12, s12)):
        rr = f1r * g[0] + f2r * h[0]
        ii = f1i * g[1] + f2i * h[1]
        ir = f1i * g[0] + f2i * h[0]
        ri = f1r * g[1] + f2r * h[1]
        re[j][k], re[k][j] = rr - ii, rr + ii
        im[j][k], im[k][j] = ir + ri, ir - ri
    return re, im


def smearing(staple, temporal):
    cr, ci = staple
    ur, ui = temporal

    def omega_re(j, k):
        t = cr[j][0] * ur[k][0] + ci[j][0] * ui[k][0]
        for m in (1, 2):
            t = t + (cr[j][m] * ur[k][m] + ci[j][m] * ui[k][m])
        return t

    def omega_im(j, k):
        t = ci[j][0] * ur[k][0] - cr[j][0] * ui[k][0]
        for m in (1, 2):
            t = t + (ci[j][m] * ur[k][m] - cr[j][m] * ui[k][m])
        return t

    half = 0.5 * SMEAR
    diag = [omega_im(j, j) for j in range(3)]
    third = (diag[0] + diag[1] + diag[2]) * (1.0 / 3.0)
    d = [(x - third) * SMEAR for x in diag]
    g = {}
    for j, k in ((0, 1), (0, 2), (1, 2)):
        g[j, k] = (
            (omega_im(j, k) + omega_im(k, j)) * half,
            (omega_re(k, j) - omega_re(j, k)) * half,
        )
    s, s01, s02, s12, q = squared(d, g[0, 1], g[0, 2], g[1, 2])
    p = (s[0] + s[1] + s[2]) * 0.5
    f1 = p * (-1.0 / 6.0) + 1.0
    f0i = q * (-1.0 / 6.0)
    re = [[None] * 3 for _ in range(3)]
    im = [[None] * 3 for _ in range(3)]
    for j in range(3):
        re[j][j] = 1.0 - 0.5 * s[j]
        im[j][j] = f0i + f1 * d[j]
    for j, k, h in ((0, 1, s01), (0, 2, s02), (1, 2, s12)):
        a = f1 * g[j, k][0]
        b = f1 * g[j, k][1]
        c = 0.5 * h[0]
        e = 0.5 * h[1]
        re[j][k], re[k][j] = -b - c, b - c
        im[j][k], im[k][j] = a - e, a + e
    return re, im


def slice_of(rows, n, t):
    return [rows[n, a, pl.ds(t, ROWS, stride=NT_LOCAL), :] for a in range(8)]


def unit():
    one = jnp.ones((ROWS, LANES), jnp.float32)
    zero = jnp.zeros((ROWS, LANES), jnp.float32)
    return (
        [[one if i == j else zero for j in range(3)] for i in range(3)],
        [[zero] * 3 for _ in range(3)],
    )


def plane_terms(spatial, temporal, ahead, above, below):
    forward = forward_term(spatial, mapped(above, temporal), ahead)
    return plus(forward, mapped(below, backward_term(spatial, temporal, ahead)))


def by_row(coeffs, rows, sems, directions):
    return [
        pltpu.make_async_copy(
            coeffs.at[direction, :, 0, :, pl.ds(v * LANES, LANES)],
            rows.at[n, :, pl.ds(v * NT_LOCAL, NT_LOCAL), :],
            sems.at[n, v],
        )
        for n, direction in enumerate(directions)
        for v in range(ROWS)
    ]


def prepare_kernel(coeffs, rows, first, sems):
    copies = by_row(coeffs, rows, sems, (0, 1, 2, 3))
    for copy in copies:
        copy.start()
    for direction in range(4):
        for copy in copies[direction * ROWS : (direction + 1) * ROWS]:
            copy.wait()
        if direction < 3:
            for a, value in enumerate(slice_of(rows, direction, 0)):
                first[direction, a] = value


def local_kernel(rows, other, links, staple, other_rows, sems):
    last = NT_LOCAL - 1
    copies = by_row(other, other_rows, sems, (0, 3))
    for copy in copies:
        copy.start()

    def make(t):
        for direction in range(4):
            write(links, link_of(slice_of(rows, direction, t)), direction, t)

    make(last)

    def step(i, carry):
        t = last - 1 - i
        make(t)
        terms = plane_terms(
            read(links, 1, t), read(links, 3, t), read(links, 1, t + 1), from_y_above, from_y_below
        )
        write(staple, terms, t)
        terms = plane_terms(
            read(links, 2, t), read(links, 3, t), read(links, 2, t + 1), from_z_above, from_z_below
        )
        write(staple, plus(read(staple, t), terms), t)
        return carry

    lax.fori_loop(0, last, step, 0)
    for copy in copies:
        copy.wait()


def chain_steps(high, low, links, staple, rows, other_links, terms, later, put):
    def step(i, carry):
        t = high - 1 - i
        write(other_links, link_of(slice_of(rows, 1, t)), 1)
        write(other_links, link_of(slice_of(rows, 0, t)), 2)
        write(
            terms,
            plus(
                read(staple, t),
                forward_term(read(links, 0, t), read(other_links, 1), read(links, 0, t + 1)),
            ),
        )
        write(
            terms,
            plus(
                read(terms),
                backward_term(read(other_links, 2), read(other_links, 1), read(other_links, 0)),
            ),
        )
        temporal = read(links, 3, t)
        smeared = mul(smearing(read(terms), temporal), temporal)
        running = mul(smeared, read(later))
        write(later, running)
        put(t, running)
        write(other_links, read(other_links, 2), 0)
        return carry

    lax.fori_loop(0, high - low, step, 0)


def late_chain_kernel(links, staple, rows, partial, other_last, other_links, terms, later):
    last = NT_LOCAL - 1
    for n in range(2):
        write(other_last, link_of(slice_of(rows, n, last)), n)
    write(other_links, read(other_last, 0), 0)
    write(later, unit())

    def put(t, product):
        write(partial, product, t - SPLIT)

    chain_steps(last, SPLIT, links, staple, rows, other_links, terms, later, put)


def early_chain_kernel(links, staple, rows, late, after, partial, other_links, terms, later):
    del after
    write(other_links, link_of(slice_of(rows, 0, SPLIT)), 0)
    write(later, read(late, 0))

    def put(t, product):
        write(partial, product, t)

    chain_steps(SPLIT, 0, links, staple, rows, other_links, terms, later, put)


def pick_kernel(ahead, after, out):
    del after
    out[...] = ahead[0]


def last_slice_kernel(links, other_last, next_rows, other_next, partial, smeared_last, total, ahead, terms):
    last = NT_LOCAL - 1
    for direction in range(3):
        write(ahead, link_of([next_rows[direction, a] for a in range(8)]), direction)
    write(ahead, link_of([other_next[a] for a in range(8)]), 3)
    temporal = read(links, 3, last)
    write(
        terms,
        plane_terms(read(links, 1, last), temporal, read(ahead, 1), from_y_above, from_y_below),
    )
    for term in (
        lambda: plane_terms(read(links, 2, last), temporal, read(ahead, 2), from_z_above, from_z_below),
        lambda: forward_term(read(links, 0, last), read(other_last, 1), read(ahead, 0)),
        lambda: backward_term(read(other_last, 0), read(other_last, 1), read(ahead, 3)),
    ):
        write(terms, plus(read(terms), term()))
    smeared = mul(smearing(read(terms), temporal), temporal)
    write(smeared_last, smeared)
    write(total, mul(read(partial, 0), read(smeared_last)))


def suffixes(low, peers, own, by1, by2, by3, held):
    digit = lax.rem(lax.axis_index("tm") // low, 4)
    for k, ref in zip((0, *peers), (own, by1, by2, by3)):
        for a in range(18):
            held[k, a] = ref[a]
    third = read(held, 3 ^ digit)
    second = mul(read(held, 2 ^ digit), third)
    first = mul(read(held, 1 ^ digit), second)
    zeroth = read(held, digit)
    for k, matrix in enumerate((first, second, third, unit())):
        write(held, matrix, 4 + k)
    return zeroth, 4 + digit


def level_kernel(low, own, by1, by2, by3, tail, new_total, new_tail, held):
    zeroth, at = suffixes(low, PEERS, own, by1, by2, by3, held)
    write(new_total, mul(zeroth, read(held, 4)))
    write(new_tail, mul(read(tail), read(held, at)))


def closing_kernel(low, own, by1, by2, by3, tail, early, late, out, held, rows, sems):
    _, at = suffixes(low, LAST_PEERS, own, by1, by2, by3, held)
    write(held, mul(read(tail), read(held, at)), 0)
    last = NT_LOCAL - 1
    copies = []
    for i in range(3):

        def put(t, row, i=i):
            for part in range(2):
                for j in range(3):
                    rows[9 * part + 3 * i + j, pl.ds(t, ROWS, stride=NT_LOCAL), :] = row[part][j]

        for partial, low, high in ((early, 0, SPLIT), (late, SPLIT, last)):

            def step(t, carry, partial=partial, low=low, i=i, put=put):
                left = [[partial[t - low, 9 * part + 3 * i + j] for j in range(3)] for part in range(2)]
                put(t, row_times(left, read(held, 0)))
                return carry

            lax.fori_loop(low, high, step, 0)
        put(last, [[held[0, 9 * part + 3 * i + j] for j in range(3)] for part in range(2)])
        for part in range(2):
            for v in range(ROWS):
                copies.append(
                    pltpu.make_async_copy(
                        rows.at[pl.ds(9 * part + 3 * i, 3), pl.ds(v * NT_LOCAL, NT_LOCAL), :],
                        out.at[pl.ds(9 * part + 3 * i, 3), :, pl.ds(v * LANES, LANES)],
                        sems.at[i, part, v],
                    )
                )
                copies[-1].start()
    for copy in copies:
        copy.wait()


def params():
    return pltpu.CompilerParams(vmem_limit_bytes=VMEM_LIMIT)


def field(*lead):
    return jax.ShapeDtypeStruct((*lead, 18, ROWS, LANES), jnp.float32)


def cost(flops):
    return pl.CostEstimate(flops=flops, bytes_accessed=1_000_000, transcendentals=0)


def block(*shape):
    return jax.ShapeDtypeStruct(shape, jnp.float32)


def shards(coeffs):
    count = lax.axis_size("tm")
    other = lax.ppermute(coeffs, "space", [(0, 1), (1, 0)])
    rows, first = pl.pallas_call(
        prepare_kernel,
        out_shape=(block(4, 8, ROWS * NT_LOCAL, LANES), block(3, 8, ROWS, LANES)),
        in_specs=[pl.BlockSpec(memory_space=pltpu.HBM)],
        out_specs=(WHOLE, WHOLE),
        scratch_shapes=[pltpu.SemaphoreType.DMA((4, ROWS))],
        compiler_params=params(),
        name="prepare",
    )(pltpu.with_memory_space_constraint(coeffs, pltpu.HBM))
    ahead = lax.ppermute(first, "tm", [((i + 1) % count, i) for i in range(count)])
    links, staple, other_rows = pl.pallas_call(
        local_kernel,
        out_shape=(field(4, NT_LOCAL), field(NT_LOCAL), block(2, 8, ROWS * NT_LOCAL, LANES)),
        in_specs=[WHOLE, WHOLE],
        out_specs=(WHOLE, WHOLE, WHOLE),
        scratch_shapes=[pltpu.SemaphoreType.DMA((2, ROWS))],
        compiler_params=params(),
        cost_estimate=cost(20_000_000),
        name="local_terms",
    )(rows, other)
    chain_scratch = [
        pltpu.VMEM((3, 18, ROWS, LANES), jnp.float32),
        pltpu.VMEM((18, ROWS, LANES), jnp.float32),
        pltpu.VMEM((18, ROWS, LANES), jnp.float32),
    ]
    late, other_last = pl.pallas_call(
        late_chain_kernel,
        out_shape=(field(NT_LOCAL - 1 - SPLIT), field(2)),
        in_specs=[WHOLE] * 3,
        out_specs=(WHOLE, WHOLE),
        scratch_shapes=chain_scratch,
        compiler_params=params(),
        cost_estimate=cost(8_000_000),
        name="late_chain",
    )(links, staple, other_rows)
    ahead_x = pl.pallas_call(
        pick_kernel,
        out_shape=block(8, ROWS, LANES),
        in_specs=[WHOLE, WHOLE],
        out_specs=WHOLE,
        compiler_params=params(),
        name="pick",
    )(ahead, late)
    other_ahead = lax.ppermute(ahead_x, "space", [(0, 1), (1, 0)])
    early = pl.pallas_call(
        early_chain_kernel,
        out_shape=field(SPLIT),
        in_specs=[WHOLE] * 5,
        out_specs=WHOLE,
        scratch_shapes=chain_scratch,
        compiler_params=params(),
        cost_estimate=cost(8_000_000),
        name="early_chain",
    )(links, staple, other_rows, late, ahead_x)
    tail, total = pl.pallas_call(
        last_slice_kernel,
        out_shape=(field(), field()),
        in_specs=[WHOLE] * 5,
        out_specs=(WHOLE, WHOLE),
        scratch_shapes=[
            pltpu.VMEM((4, 18, ROWS, LANES), jnp.float32),
            pltpu.VMEM((18, ROWS, LANES), jnp.float32),
        ],
        compiler_params=params(),
        cost_estimate=cost(5_000_000),
        name="last_slice",
    )(links, other_last, ahead, other_ahead, early)
    low = 1
    while True:
        peers = LAST_PEERS if low * 4 >= count else PEERS
        received = [
            lax.ppermute(total, "tm", [(i, i ^ (low * k)) for i in range(count)]) for k in peers
        ]
        held = pltpu.VMEM((8, 18, ROWS, LANES), jnp.float32)
        if low * 4 >= count:
            break

        def level(*refs, low=low):
            level_kernel(low, *refs)

        total, tail = pl.pallas_call(
            level,
            out_shape=(field(), field()),
            in_specs=[WHOLE] * 5,
            out_specs=(WHOLE, WHOLE),
            scratch_shapes=[held],
            compiler_params=params(),
            name=f"level_{low}",
        )(total, *received, tail)
        low *= 4

    def closing(*refs, low=low):
        closing_kernel(low, *refs)

    out = pl.pallas_call(
        closing,
        out_shape=jax.ShapeDtypeStruct((18, NT_LOCAL, ROWS * LANES), jnp.float32),
        in_specs=[WHOLE] * 7,
        out_specs=pl.BlockSpec(memory_space=pltpu.HBM),
        scratch_shapes=[
            held,
            pltpu.VMEM((18, ROWS * NT_LOCAL, LANES), jnp.float32),
            pltpu.SemaphoreType.DMA((3, 2, ROWS)),
        ],
        compiler_params=params(),
        name="closing",
    )(total, *received, tail, early, late)
    return out.reshape(2, 3, 3, 1, NT_LOCAL, ROWS * LANES)


def solution(mesh):
    in_specs = (P(None, None, "space", "tm", None),)
    out_specs = P(None, None, None, "space", "tm", None)
    return jax.shard_map(shards, mesh=mesh, in_specs=in_specs, out_specs=out_specs, check_vma=False)
```

```python
import jax
import jax.numpy as jnp
from jax import lax
from jax.experimental import pallas as pl
from jax.experimental.pallas import tpu as pltpu
from jax.sharding import PartitionSpec as P

ZDIM = 32
LANES = 128
ROWS = 8
NT_LOCAL = 8
SMEAR = 0.1
SPLIT = 2
PEERS = (2, 3, 1)
LAST_PEERS = (1, 2, 3)
ROOT_THIRD = 1.0 / 3.0**0.5
VMEM_LIMIT = 48 * 1024 * 1024
WHOLE = pl.BlockSpec(memory_space=pltpu.VMEM)


def read(ref, *index):
    re = [[ref[(*index, 3 * i + j)] for j in range(3)] for i in range(3)]
    im = [[ref[(*index, 9 + 3 * i + j)] for j in range(3)] for i in range(3)]
    return re, im


def write(ref, matrix, *index):
    for part in range(2):
        for i in range(3):
            for j in range(3):
                ref[(*index, 9 * part + 3 * i + j)] = matrix[part][i][j]


def row_times(row, matrix, conj_left=False, conj_right=False):
    a, b = row
    c, d = matrix
    out_re, out_im = [], []
    for j in range(3):
        rr = a[0] * c[0][j]
        ii = b[0] * d[0][j]
        ri = a[0] * d[0][j]
        ir = b[0] * c[0][j]
        for m in (1, 2):
            rr = rr + a[m] * c[m][j]
            ii = ii + b[m] * d[m][j]
            ri = ri + a[m] * d[m][j]
            ir = ir + b[m] * c[m][j]
        out_re.append(rr + ii if conj_left != conj_right else rr - ii)
        if conj_left and conj_right:
            out_im.append(-(ri + ir))
        elif conj_left:
            out_im.append(ri - ir)
        elif conj_right:
            out_im.append(ir - ri)
        else:
            out_im.append(ri + ir)
    return out_re, out_im


def mul(left, right):
    re, im = [], []
    for i in range(3):
        r, m = row_times((left[0][i], left[1][i]), right)
        re.append(r)
        im.append(m)
    return re, im


def transposed(matrix):
    return tuple([[part[j][i] for j in range(3)] for i in range(3)] for part in matrix)


def forward_term(link, temporal, ahead):
    turned = transposed(ahead)
    re, im = [], []
    for i in range(3):
        row = row_times((link[0][i], link[1][i]), temporal)
        r, m = row_times(row, turned, conj_right=True)
        re.append(r)
        im.append(m)
    return re, im


def backward_term(link, temporal, ahead):
    turned = transposed(link)
    re, im = [], []
    for i in range(3):
        row = row_times((turned[0][i], turned[1][i]), temporal, conj_left=True)
        r, m = row_times(row, ahead)
        re.append(r)
        im.append(m)
    return re, im


def plus(left, right):
    return tuple(
        [[left[p][i][j] + right[p][i][j] for j in range(3)] for i in range(3)] for p in range(2)
    )


def mapped(f, matrix):
    return tuple([[f(part[i][j]) for j in range(3)] for i in range(3)] for part in matrix)


def lane():
    return lax.broadcasted_iota(jnp.int32, (ROWS, LANES), 1)


def from_y_above(x):
    r = pltpu.roll(x, LANES - ZDIM, 1)
    return jnp.where(lane() >= LANES - ZDIM, pltpu.roll(r, ROWS - 1, 0), r)


def from_y_below(x):
    r = pltpu.roll(x, ZDIM, 1)
    return jnp.where(lane() < ZDIM, pltpu.roll(r, 1, 0), r)


def from_z_above(x):
    edge = lane() % ZDIM == ZDIM - 1
    return jnp.where(edge, pltpu.roll(x, ZDIM - 1, 1), pltpu.roll(x, LANES - 1, 1))


def from_z_below(x):
    edge = lane() % ZDIM == 0
    return jnp.where(edge, pltpu.roll(x, LANES - ZDIM + 1, 1), pltpu.roll(x, 1, 1))


def squared(d, g01, g02, g12):
    n01 = g01[0] * g01[0] + g01[1] * g01[1]
    n02 = g02[0] * g02[0] + g02[1] * g02[1]
    n12 = g12[0] * g12[0] + g12[1] * g12[1]
    s = (d[0] * d[0] + (n01 + n02), d[1] * d[1] + (n01 + n12), d[2] * d[2] + (n02 + n12))
    k = (g01[0] * g12[0] - g01[1] * g12[1], g01[0] * g12[1] + g01[1] * g12[0])
    s02 = (k[0] - d[1] * g02[0], k[1] - d[1] * g02[1])
    s01 = (
        (g02[0] * g12[0] + g02[1] * g12[1]) - d[2] * g01[0],
        (g02[1] * g12[0] - g02[0] * g12[1]) - d[2] * g01[1],
    )
    s12 = (
        (g01[0] * g02[0] + g01[1] * g02[1]) - d[0] * g12[0],
        (g01[0] * g02[1] - g01[1] * g02[0]) - d[0] * g12[1],
    )
    det = (
        d[0] * (d[1] * d[2] - n12)
        - d[1] * n02
        - d[2] * n01
        + 2.0 * (k[0] * g02[0] + k[1] * g02[1])
    )
    return s, s01, s02, s12, det


def link_of(c):
    d2 = c[7] * (-2.0 * ROOT_THIRD)
    e = c[7] * ROOT_THIRD
    d = (e + c[2], e - c[2], d2)
    g01, g02, g12 = (c[0], -c[1]), (c[3], -c[4]), (c[5], -c[6])
    s, s01, s02, s12, det = squared(d, g01, g02, g12)
    p = (s[0] + s[1] + s[2]) * 0.125
    q = det * 0.125
    qq = q * q
    w = (p * (-1.0 / 5040.0) + 1.0 / 120.0) * p - 1.0 / 6.0
    f0r = qq * (p * (1.0 / 20160.0) - 1.0 / 720.0) + 1.0
    f0i = q * w
    f1r = q * ((p * (0.5 / 13440.0) - 0.5 / 360.0) * p + 0.5 / 24.0)
    f1i = (p * w + qq * (-1.0 / 5040.0)) * 0.5 + 0.5
    f2r = ((p * (0.25 / 40320.0) - 0.25 / 720.0) * p + 0.25 / 24.0) * p + (qq * (0.25 / 40320.0) - 0.125)
    f2i = q * (p * (-0.5 / 5040.0) + 0.25 / 120.0)
    re = [[None] * 3 for _ in range(3)]
    im = [[None] * 3 for _ in range(3)]
    for j in range(3):
        re[j][j] = f0r + (f1r * d[j] + f2r * s[j])
        im[j][j] = f0i + (f1i * d[j] + f2i * s[j])
    for j, k, g, h in ((0, 1, g01, s01), (0, 2, g02, s02), (1, 2, g12, s12)):
        rr = f1r * g[0] + f2r * h[0]
        ii = f1i * g[1] + f2i * h[1]
        ir = f1i * g[0] + f2i * h[0]
        ri = f1r * g[1] + f2r * h[1]
        re[j][k], re[k][j] = rr - ii, rr + ii
        im[j][k], im[k][j] = ir + ri, ir - ri
    return re, im


def smearing(staple, temporal):
    cr, ci = staple
    ur, ui = temporal

    def omega_re(j, k):
        t = cr[j][0] * ur[k][0] + ci[j][0] * ui[k][0]
        for m in (1, 2):
            t = t + (cr[j][m] * ur[k][m] + ci[j][m] * ui[k][m])
        return t

    def omega_im(j, k):
        t = ci[j][0] * ur[k][0] - cr[j][0] * ui[k][0]
        for m in (1, 2):
            t = t + (ci[j][m] * ur[k][m] - cr[j][m] * ui[k][m])
        return t

    half = 0.5 * SMEAR
    diag = [omega_im(j, j) for j in range(3)]
    third = (diag[0] + diag[1] + diag[2]) * (1.0 / 3.0)
    d = [(x - third) * SMEAR for x in diag]
    g = {}
    for j, k in ((0, 1), (0, 2), (1, 2)):
        g[j, k] = (
            (omega_im(j, k) + omega_im(k, j)) * half,
            (omega_re(k, j) - omega_re(j, k)) * half,
        )
    s, s01, s02, s12, q = squared(d, g[0, 1], g[0, 2], g[1, 2])
    p = (s[0] + s[1] + s[2]) * 0.5
    f1 = p * (-1.0 / 6.0) + 1.0
    f0i = q * (-1.0 / 6.0)
    re = [[None] * 3 for _ in range(3)]
    im = [[None] * 3 for _ in range(3)]
    for j in range(3):
        re[j][j] = 1.0 - 0.5 * s[j]
        im[j][j] = f0i + f1 * d[j]
    for j, k, h in ((0, 1, s01), (0, 2, s02), (1, 2, s12)):
        a = f1 * g[j, k][0]
        b = f1 * g[j, k][1]
        c = 0.5 * h[0]
        e = 0.5 * h[1]
        re[j][k], re[k][j] = -b - c, b - c
        im[j][k], im[k][j] = a - e, a + e
    return re, im


def slice_of(rows, n, t):
    return [rows[n, a, pl.ds(t, ROWS, stride=NT_LOCAL), :] for a in range(8)]


def unit():
    one = jnp.ones((ROWS, LANES), jnp.float32)
    zero = jnp.zeros((ROWS, LANES), jnp.float32)
    return (
        [[one if i == j else zero for j in range(3)] for i in range(3)],
        [[zero] * 3 for _ in range(3)],
    )


def plane_terms(spatial, temporal, ahead, above, below):
    forward = forward_term(spatial, mapped(above, temporal), ahead)
    return plus(forward, mapped(below, backward_term(spatial, temporal, ahead)))


def prepare_kernel(coeffs, rows, first, sems):
    copies = [pltpu.make_async_copy(coeffs.at[n], rows.at[n], sems.at[n]) for n in range(4)]
    for copy in copies:
        copy.start()
    for direction in range(4):
        copies[direction].wait()
        if direction < 3:
            for a, value in enumerate(slice_of(rows, direction, 0)):
                first[direction, a] = value


def local_kernel(rows, links, staple):
    last = NT_LOCAL - 1

    def make(t):
        for direction in range(4):
            write(links, link_of(slice_of(rows, direction, t)), direction, t)

    make(last)

    def step(i, carry):
        t = last - 1 - i
        make(t)
        terms = plane_terms(
            read(links, 1, t), read(links, 3, t), read(links, 1, t + 1), from_y_above, from_y_below
        )
        write(staple, terms, t)
        terms = plane_terms(
            read(links, 2, t), read(links, 3, t), read(links, 2, t + 1), from_z_above, from_z_below
        )
        write(staple, plus(read(staple, t), terms), t)
        return carry

    lax.fori_loop(0, last, step, 0)


def chain_steps(high, low, links, staple, rows, other_links, terms, later, put):
    def step(i, carry):
        t = high - 1 - i
        write(other_links, link_of(slice_of(rows, 3, t)), 1)
        write(other_links, link_of(slice_of(rows, 0, t)), 2)
        write(
            terms,
            plus(
                read(staple, t),
                forward_term(read(links, 0, t), read(other_links, 1), read(links, 0, t + 1)),
            ),
        )
        write(
            terms,
            plus(
                read(terms),
                backward_term(read(other_links, 2), read(other_links, 1), read(other_links, 0)),
            ),
        )
        temporal = read(links, 3, t)
        smeared = mul(smearing(read(terms), temporal), temporal)
        running = mul(smeared, read(later))
        write(later, running)
        put(t, running)
        write(other_links, read(other_links, 2), 0)
        return carry

    lax.fori_loop(0, high - low, step, 0)


def late_chain_kernel(links, staple, rows, partial, other_last, other_links, terms, later):
    last = NT_LOCAL - 1
    for n, direction in enumerate((0, 3)):
        write(other_last, link_of(slice_of(rows, direction, last)), n)
    write(other_links, read(other_last, 0), 0)
    write(later, unit())

    def put(t, product):
        write(partial, product, t - SPLIT)

    chain_steps(last, SPLIT, links, staple, rows, other_links, terms, later, put)


def early_chain_kernel(
    links, staple, rows, late, other_last, next_rows, partial, last_terms, other_links, terms, later, ahead
):
    write(other_links, link_of(slice_of(rows, 0, SPLIT)), 0)
    write(later, read(late, 0))

    def put(t, product):
        write(partial, product, t)

    chain_steps(SPLIT, 0, links, staple, rows, other_links, terms, later, put)
    last = NT_LOCAL - 1
    for direction in range(3):
        write(ahead, link_of([next_rows[direction, a] for a in range(8)]), direction)
    temporal = read(links, 3, last)
    write(
        last_terms,
        plane_terms(read(links, 1, last), temporal, read(ahead, 1), from_y_above, from_y_below),
    )
    for term in (
        lambda: plane_terms(read(links, 2, last), temporal, read(ahead, 2), from_z_above, from_z_below),
        lambda: forward_term(read(links, 0, last), read(other_last, 1), read(ahead, 0)),
    ):
        write(last_terms, plus(read(last_terms), term()))


def pick_kernel(ahead, after, out):
    del after
    out[...] = ahead[0]


def last_slice_kernel(links, other_last, last_terms, other_next, partial, smeared_last, total, ahead):
    write(ahead, link_of([other_next[a] for a in range(8)]))
    temporal = read(links, 3, NT_LOCAL - 1)
    terms = plus(
        read(last_terms), backward_term(read(other_last, 0), read(other_last, 1), read(ahead))
    )
    write(ahead, terms)
    smeared = mul(smearing(read(ahead), temporal), temporal)
    write(smeared_last, smeared)
    write(total, mul(read(partial, 0), read(smeared_last)))


def suffixes(low, peers, own, by1, by2, by3, held):
    digit = lax.rem(lax.axis_index("tm") // low, 4)
    for k, ref in zip((0, *peers), (own, by1, by2, by3)):
        for a in range(18):
            held[k, a] = ref[a]
    third = read(held, 3 ^ digit)
    second = mul(read(held, 2 ^ digit), third)
    first = mul(read(held, 1 ^ digit), second)
    zeroth = read(held, digit)
    for k, matrix in enumerate((first, second, third, unit())):
        write(held, matrix, 4 + k)
    return zeroth, 4 + digit


def level_kernel(low, own, by1, by2, by3, tail, new_total, new_tail, held):
    zeroth, at = suffixes(low, PEERS, own, by1, by2, by3, held)
    write(new_total, mul(zeroth, read(held, 4)))
    write(new_tail, mul(read(tail), read(held, at)))


def closing_kernel(low, own, by1, by2, by3, tail, early, late, out, held, rows, sems):
    _, at = suffixes(low, LAST_PEERS, own, by1, by2, by3, held)
    write(held, mul(read(tail), read(held, at)), 0)
    last = NT_LOCAL - 1
    copies = []
    for i in range(3):

        def put(t, row, i=i):
            for part in range(2):
                for j in range(3):
                    rows[9 * part + 3 * i + j, pl.ds(t, ROWS, stride=NT_LOCAL), :] = row[part][j]

        for partial, low, high in ((early, 0, SPLIT), (late, SPLIT, last)):

            def step(t, carry, partial=partial, low=low, i=i, put=put):
                left = [[partial[t - low, 9 * part + 3 * i + j] for j in range(3)] for part in range(2)]
                put(t, row_times(left, read(held, 0)))
                return carry

            lax.fori_loop(low, high, step, 0)
        put(last, [[held[0, 9 * part + 3 * i + j] for j in range(3)] for part in range(2)])
        for part in range(2):
            planes = pl.ds(9 * part + 3 * i, 3)
            copies.append(pltpu.make_async_copy(rows.at[planes], out.at[planes], sems.at[i, part]))
            copies[-1].start()
    for copy in copies:
        copy.wait()


def params():
    return pltpu.CompilerParams(vmem_limit_bytes=VMEM_LIMIT)


def field(*lead):
    return jax.ShapeDtypeStruct((*lead, 18, ROWS, LANES), jnp.float32)


def cost(flops):
    return pl.CostEstimate(flops=flops, bytes_accessed=1_000_000, transcendentals=0)


def block(*shape):
    return jax.ShapeDtypeStruct(shape, jnp.float32)


def shards(coeffs):
    count = lax.axis_size("tm")
    coeffs = coeffs.reshape(4, 8, NT_LOCAL, ROWS, LANES).swapaxes(2, 3)
    coeffs = coeffs.reshape(4, 8, ROWS * NT_LOCAL, LANES)
    other_rows = lax.ppermute(coeffs, "space", [(0, 1), (1, 0)])
    rows, first = pl.pallas_call(
        prepare_kernel,
        out_shape=(block(4, 8, ROWS * NT_LOCAL, LANES), block(3, 8, ROWS, LANES)),
        in_specs=[pl.BlockSpec(memory_space=pltpu.HBM)],
        out_specs=(WHOLE, WHOLE),
        scratch_shapes=[pltpu.SemaphoreType.DMA((4,))],
        compiler_params=params(),
        name="prepare",
    )(pltpu.with_memory_space_constraint(coeffs, pltpu.HBM))
    ahead = lax.ppermute(first, "tm", [((i + 1) % count, i) for i in range(count)])
    links, staple = pl.pallas_call(
        local_kernel,
        out_shape=(field(4, NT_LOCAL), field(NT_LOCAL)),
        in_specs=[WHOLE],
        out_specs=(WHOLE, WHOLE),
        compiler_params=params(),
        cost_estimate=cost(20_000_000),
        name="local_terms",
    )(rows)
    chain_scratch = [
        pltpu.VMEM((3, 18, ROWS, LANES), jnp.float32),
        pltpu.VMEM((18, ROWS, LANES), jnp.float32),
        pltpu.VMEM((18, ROWS, LANES), jnp.float32),
    ]
    late, other_last = pl.pallas_call(
        late_chain_kernel,
        out_shape=(field(NT_LOCAL - 1 - SPLIT), field(2)),
        in_specs=[WHOLE] * 3,
        out_specs=(WHOLE, WHOLE),
        scratch_shapes=chain_scratch,
        compiler_params=params(),
        cost_estimate=cost(8_000_000),
        name="late_chain",
    )(links, staple, other_rows)
    ahead_x = pl.pallas_call(
        pick_kernel,
        out_shape=block(8, ROWS, LANES),
        in_specs=[WHOLE, WHOLE],
        out_specs=WHOLE,
        compiler_params=params(),
        name="pick",
    )(ahead, late)
    other_ahead = lax.ppermute(ahead_x, "space", [(0, 1), (1, 0)])
    early, last_terms = pl.pallas_call(
        early_chain_kernel,
        out_shape=(field(SPLIT), field()),
        in_specs=[WHOLE] * 6,
        out_specs=(WHOLE, WHOLE),
        scratch_shapes=chain_scratch + [pltpu.VMEM((3, 18, ROWS, LANES), jnp.float32)],
        compiler_params=params(),
        cost_estimate=cost(8_000_000),
        name="early_chain",
    )(links, staple, other_rows, late, other_last, ahead)
    tail, total = pl.pallas_call(
        last_slice_kernel,
        out_shape=(field(), field()),
        in_specs=[WHOLE] * 5,
        out_specs=(WHOLE, WHOLE),
        scratch_shapes=[pltpu.VMEM((18, ROWS, LANES), jnp.float32)],
        compiler_params=params(),
        cost_estimate=cost(3_000_000),
        name="last_slice",
    )(links, other_last, last_terms, other_ahead, early)
    low = 1
    while True:
        peers = LAST_PEERS if low * 4 >= count else PEERS
        received = [
            lax.ppermute(total, "tm", [(i, i ^ (low * k)) for i in range(count)]) for k in peers
        ]
        held = pltpu.VMEM((8, 18, ROWS, LANES), jnp.float32)
        if low * 4 >= count:
            break

        def level(*refs, low=low):
            level_kernel(low, *refs)

        total, tail = pl.pallas_call(
            level,
            out_shape=(field(), field()),
            in_specs=[WHOLE] * 5,
            out_specs=(WHOLE, WHOLE),
            scratch_shapes=[held],
            compiler_params=params(),
            name=f"level_{low}",
        )(total, *received, tail)
        low *= 4

    def closing(*refs, low=low):
        closing_kernel(low, *refs)

    out = pl.pallas_call(
        closing,
        out_shape=block(18, ROWS * NT_LOCAL, LANES),
        in_specs=[WHOLE] * 7,
        out_specs=pl.BlockSpec(memory_space=pltpu.HBM),
        scratch_shapes=[
            held,
            pltpu.VMEM((18, ROWS * NT_LOCAL, LANES), jnp.float32),
            pltpu.SemaphoreType.DMA((3, 2)),
        ],
        compiler_params=params(),
        name="closing",
    )(total, *received, tail, early, late)
    out = out.reshape(18, ROWS, NT_LOCAL, LANES).swapaxes(1, 2)
    return out.reshape(2, 3, 3, 1, NT_LOCAL, ROWS * LANES)


def solution(mesh):
    in_specs = (P(None, None, "space", "tm", None),)
    out_specs = P(None, None, None, "space", "tm", None)
    return jax.shard_map(shards, mesh=mesh, in_specs=in_specs, out_specs=out_specs, check_vma=False)
```

```python
import jax
import jax.numpy as jnp
from jax import lax
from jax.experimental import pallas as pl
from jax.experimental.pallas import tpu as pltpu
from jax.sharding import PartitionSpec as P

ZDIM = 32
LANES = 128
ROWS = 8
NT_LOCAL = 8
SMEAR = 0.1
SPLIT = 2
PEERS = (2, 3, 1)
LAST_PEERS = (1, 2, 3)
ROOT_THIRD = 1.0 / 3.0**0.5
VMEM_LIMIT = 48 * 1024 * 1024
WHOLE = pl.BlockSpec(memory_space=pltpu.VMEM)


def read(ref, *index):
    re = [[ref[(*index, 3 * i + j)] for j in range(3)] for i in range(3)]
    im = [[ref[(*index, 9 + 3 * i + j)] for j in range(3)] for i in range(3)]
    return re, im


def write(ref, matrix, *index):
    for part in range(2):
        for i in range(3):
            for j in range(3):
                ref[(*index, 9 * part + 3 * i + j)] = matrix[part][i][j]


def row_times(row, matrix, conj_left=False, conj_right=False):
    a, b = row
    c, d = matrix
    out_re, out_im = [], []
    for j in range(3):
        rr = a[0] * c[0][j]
        ii = b[0] * d[0][j]
        ri = a[0] * d[0][j]
        ir = b[0] * c[0][j]
        for m in (1, 2):
            rr = rr + a[m] * c[m][j]
            ii = ii + b[m] * d[m][j]
            ri = ri + a[m] * d[m][j]
            ir = ir + b[m] * c[m][j]
        out_re.append(rr + ii if conj_left != conj_right else rr - ii)
        if conj_left and conj_right:
            out_im.append(-(ri + ir))
        elif conj_left:
            out_im.append(ri - ir)
        elif conj_right:
            out_im.append(ir - ri)
        else:
            out_im.append(ri + ir)
    return out_re, out_im


def mul(left, right):
    re, im = [], []
    for i in range(3):
        r, m = row_times((left[0][i], left[1][i]), right)
        re.append(r)
        im.append(m)
    return re, im


def transposed(matrix):
    return tuple([[part[j][i] for j in range(3)] for i in range(3)] for part in matrix)


def forward_term(link, temporal, ahead):
    turned = transposed(ahead)
    re, im = [], []
    for i in range(3):
        row = row_times((link[0][i], link[1][i]), temporal)
        r, m = row_times(row, turned, conj_right=True)
        re.append(r)
        im.append(m)
    return re, im


def backward_term(link, temporal, ahead):
    turned = transposed(link)
    re, im = [], []
    for i in range(3):
        row = row_times((turned[0][i], turned[1][i]), temporal, conj_left=True)
        r, m = row_times(row, ahead)
        re.append(r)
        im.append(m)
    return re, im


def plus(left, right):
    return tuple(
        [[left[p][i][j] + right[p][i][j] for j in range(3)] for i in range(3)] for p in range(2)
    )


def mapped(f, matrix):
    return tuple([[f(part[i][j]) for j in range(3)] for i in range(3)] for part in matrix)


def lane():
    return lax.broadcasted_iota(jnp.int32, (ROWS, LANES), 1)


def from_y_above(x):
    r = pltpu.roll(x, LANES - ZDIM, 1)
    return jnp.where(lane() >= LANES - ZDIM, pltpu.roll(r, ROWS - 1, 0), r)


def from_y_below(x):
    r = pltpu.roll(x, ZDIM, 1)
    return jnp.where(lane() < ZDIM, pltpu.roll(r, 1, 0), r)


def from_z_above(x):
    edge = lane() % ZDIM == ZDIM - 1
    return jnp.where(edge, pltpu.roll(x, ZDIM - 1, 1), pltpu.roll(x, LANES - 1, 1))


def from_z_below(x):
    edge = lane() % ZDIM == 0
    return jnp.where(edge, pltpu.roll(x, LANES - ZDIM + 1, 1), pltpu.roll(x, 1, 1))


def squared(d, g01, g02, g12):
    n01 = g01[0] * g01[0] + g01[1] * g01[1]
    n02 = g02[0] * g02[0] + g02[1] * g02[1]
    n12 = g12[0] * g12[0] + g12[1] * g12[1]
    s = (d[0] * d[0] + (n01 + n02), d[1] * d[1] + (n01 + n12), d[2] * d[2] + (n02 + n12))
    k = (g01[0] * g12[0] - g01[1] * g12[1], g01[0] * g12[1] + g01[1] * g12[0])
    s02 = (k[0] - d[1] * g02[0], k[1] - d[1] * g02[1])
    s01 = (
        (g02[0] * g12[0] + g02[1] * g12[1]) - d[2] * g01[0],
        (g02[1] * g12[0] - g02[0] * g12[1]) - d[2] * g01[1],
    )
    s12 = (
        (g01[0] * g02[0] + g01[1] * g02[1]) - d[0] * g12[0],
        (g01[0] * g02[1] - g01[1] * g02[0]) - d[0] * g12[1],
    )
    det = (
        d[0] * (d[1] * d[2] - n12)
        - d[1] * n02
        - d[2] * n01
        + 2.0 * (k[0] * g02[0] + k[1] * g02[1])
    )
    return s, s01, s02, s12, det


def link_of(c):
    d2 = c[7] * (-2.0 * ROOT_THIRD)
    e = c[7] * ROOT_THIRD
    d = (e + c[2], e - c[2], d2)
    g01, g02, g12 = (c[0], -c[1]), (c[3], -c[4]), (c[5], -c[6])
    s, s01, s02, s12, det = squared(d, g01, g02, g12)
    p = (s[0] + s[1] + s[2]) * 0.125
    q = det * 0.125
    qq = q * q
    w = (p * (-1.0 / 5040.0) + 1.0 / 120.0) * p - 1.0 / 6.0
    f0r = qq * (p * (1.0 / 20160.0) - 1.0 / 720.0) + 1.0
    f0i = q * w
    f1r = q * ((p * (0.5 / 13440.0) - 0.5 / 360.0) * p + 0.5 / 24.0)
    f1i = (p * w + qq * (-1.0 / 5040.0)) * 0.5 + 0.5
    f2r = ((p * (0.25 / 40320.0) - 0.25 / 720.0) * p + 0.25 / 24.0) * p + (qq * (0.25 / 40320.0) - 0.125)
    f2i = q * (p * (-0.5 / 5040.0) + 0.25 / 120.0)
    re = [[None] * 3 for _ in range(3)]
    im = [[None] * 3 for _ in range(3)]
    for j in range(3):
        re[j][j] = f0r + (f1r * d[j] + f2r * s[j])
        im[j][j] = f0i + (f1i * d[j] + f2i * s[j])
    for j, k, g, h in ((0, 1, g01, s01), (0, 2, g02, s02), (1, 2, g12, s12)):
        rr = f1r * g[0] + f2r * h[0]
        ii = f1i * g[1] + f2i * h[1]
        ir = f1i * g[0] + f2i * h[0]
        ri = f1r * g[1] + f2r * h[1]
        re[j][k], re[k][j] = rr - ii, rr + ii
        im[j][k], im[k][j] = ir + ri, ir - ri
    return re, im


def smearing(staple, temporal):
    cr, ci = staple
    ur, ui = temporal

    def omega_re(j, k):
        t = cr[j][0] * ur[k][0] + ci[j][0] * ui[k][0]
        for m in (1, 2):
            t = t + (cr[j][m] * ur[k][m] + ci[j][m] * ui[k][m])
        return t

    def omega_im(j, k):
        t = ci[j][0] * ur[k][0] - cr[j][0] * ui[k][0]
        for m in (1, 2):
            t = t + (ci[j][m] * ur[k][m] - cr[j][m] * ui[k][m])
        return t

    half = 0.5 * SMEAR
    diag = [omega_im(j, j) for j in range(3)]
    third = (diag[0] + diag[1] + diag[2]) * (1.0 / 3.0)
    d = [(x - third) * SMEAR for x in diag]
    g = {}
    for j, k in ((0, 1), (0, 2), (1, 2)):
        g[j, k] = (
            (omega_im(j, k) + omega_im(k, j)) * half,
            (omega_re(k, j) - omega_re(j, k)) * half,
        )
    s, s01, s02, s12, q = squared(d, g[0, 1], g[0, 2], g[1, 2])
    p = (s[0] + s[1] + s[2]) * 0.5
    f1 = p * (-1.0 / 6.0) + 1.0
    f0i = q * (-1.0 / 6.0)
    re = [[None] * 3 for _ in range(3)]
    im = [[None] * 3 for _ in range(3)]
    for j in range(3):
        re[j][j] = 1.0 - 0.5 * s[j]
        im[j][j] = f0i + f1 * d[j]
    for j, k, h in ((0, 1, s01), (0, 2, s02), (1, 2, s12)):
        a = f1 * g[j, k][0]
        b = f1 * g[j, k][1]
        c = 0.5 * h[0]
        e = 0.5 * h[1]
        re[j][k], re[k][j] = -b - c, b - c
        im[j][k], im[k][j] = a - e, a + e
    return re, im


def slice_of(rows, n, t):
    return [rows[n, a, pl.ds(t, ROWS, stride=NT_LOCAL), :] for a in range(8)]


def unit():
    one = jnp.ones((ROWS, LANES), jnp.float32)
    zero = jnp.zeros((ROWS, LANES), jnp.float32)
    return (
        [[one if i == j else zero for j in range(3)] for i in range(3)],
        [[zero] * 3 for _ in range(3)],
    )


def plane_terms(spatial, temporal, ahead, above, below):
    forward = forward_term(spatial, mapped(above, temporal), ahead)
    return plus(forward, mapped(below, backward_term(spatial, temporal, ahead)))


def local_terms(rows, links, staple):
    last = NT_LOCAL - 1

    def make(t):
        for direction in range(4):
            write(links, link_of(slice_of(rows, direction, t)), direction, t)

    make(last)

    def step(i, carry):
        t = last - 1 - i
        make(t)
        terms = plane_terms(
            read(links, 1, t), read(links, 3, t), read(links, 1, t + 1), from_y_above, from_y_below
        )
        write(staple, terms, t)
        terms = plane_terms(
            read(links, 2, t), read(links, 3, t), read(links, 2, t + 1), from_z_above, from_z_below
        )
        write(staple, plus(read(staple, t), terms), t)
        return carry

    lax.fori_loop(0, last, step, 0)


def first_kernel(coeffs, coeffs_by_row, first, links, staple, rows, sem):
    copy = pltpu.make_async_copy(coeffs.at[pl.ds(0, 3), :, :, 0, :], first, sem)
    copy.start()
    copy.wait()

    @pl.when(lax.axis_index("tm") == 0)
    def _():
        fetch = pltpu.make_async_copy(coeffs_by_row, rows, sem)
        fetch.start()
        fetch.wait()
        local_terms(rows, links, staple)


def local_kernel(rows, links_before, staple_before, links, staple):
    del links_before, staple_before

    @pl.when(lax.axis_index("tm") != 0)
    def _():
        local_terms(rows, links, staple)


def chain_steps(high, low, links, staple, rows, other_links, terms, later, put):
    def step(i, carry):
        t = high - 1 - i
        write(other_links, link_of(slice_of(rows, 3, t)), 1)
        write(other_links, link_of(slice_of(rows, 0, t)), 2)
        write(
            terms,
            plus(
                read(staple, t),
                forward_term(read(links, 0, t), read(other_links, 1), read(links, 0, t + 1)),
            ),
        )
        write(
            terms,
            plus(
                read(terms),
                backward_term(read(other_links, 2), read(other_links, 1), read(other_links, 0)),
            ),
        )
        temporal = read(links, 3, t)
        smeared = mul(smearing(read(terms), temporal), temporal)
        running = mul(smeared, read(later))
        write(later, running)
        put(t, running)
        write(other_links, read(other_links, 2), 0)
        return carry

    lax.fori_loop(0, high - low, step, 0)


def late_chain_kernel(links, staple, rows, partial, other_last, other_links, terms, later):
    last = NT_LOCAL - 1
    for n, direction in enumerate((0, 3)):
        write(other_last, link_of(slice_of(rows, direction, last)), n)
    write(other_links, read(other_last, 0), 0)
    write(later, unit())

    def put(t, product):
        write(partial, product, t - SPLIT)

    chain_steps(last, SPLIT, links, staple, rows, other_links, terms, later, put)


def early_chain_kernel(
    links, staple, rows, late, other_last, next_rows, partial, last_terms, other_links, terms, later, ahead
):
    write(other_links, link_of(slice_of(rows, 0, SPLIT)), 0)
    write(later, read(late, 0))

    def put(t, product):
        write(partial, product, t)

    chain_steps(SPLIT, 0, links, staple, rows, other_links, terms, later, put)
    last = NT_LOCAL - 1
    for direction in range(3):
        write(ahead, link_of([next_rows[direction, a] for a in range(8)]), direction)
    temporal = read(links, 3, last)
    write(
        last_terms,
        plane_terms(read(links, 1, last), temporal, read(ahead, 1), from_y_above, from_y_below),
    )
    for term in (
        lambda: plane_terms(read(links, 2, last), temporal, read(ahead, 2), from_z_above, from_z_below),
        lambda: forward_term(read(links, 0, last), read(other_last, 1), read(ahead, 0)),
    ):
        write(last_terms, plus(read(last_terms), term()))


def pick_kernel(ahead, after, out):
    del after
    out[...] = ahead[0]


def last_slice_kernel(links, other_last, last_terms, other_next, partial, smeared_last, total, ahead):
    write(ahead, link_of([other_next[a] for a in range(8)]))
    temporal = read(links, 3, NT_LOCAL - 1)
    terms = plus(
        read(last_terms), backward_term(read(other_last, 0), read(other_last, 1), read(ahead))
    )
    write(ahead, terms)
    smeared = mul(smearing(read(ahead), temporal), temporal)
    write(smeared_last, smeared)
    write(total, mul(read(partial, 0), read(smeared_last)))


def suffixes(low, peers, own, by1, by2, by3, held):
    digit = lax.rem(lax.axis_index("tm") // low, 4)
    for k, ref in zip((0, *peers), (own, by1, by2, by3)):
        for a in range(18):
            held[k, a] = ref[a]
    third = read(held, 3 ^ digit)
    second = mul(read(held, 2 ^ digit), third)
    first = mul(read(held, 1 ^ digit), second)
    zeroth = read(held, digit)
    for k, matrix in enumerate((first, second, third, unit())):
        write(held, matrix, 4 + k)
    return zeroth, 4 + digit


def level_kernel(low, own, by1, by2, by3, tail, new_total, new_tail, held):
    zeroth, at = suffixes(low, PEERS, own, by1, by2, by3, held)
    write(new_total, mul(zeroth, read(held, 4)))
    write(new_tail, mul(read(tail), read(held, at)))


def closing_kernel(low, own, by1, by2, by3, tail, early, late, out, held, rows, sems):
    _, at = suffixes(low, LAST_PEERS, own, by1, by2, by3, held)
    write(held, mul(read(tail), read(held, at)), 0)
    last = NT_LOCAL - 1
    copies = []
    for i in range(3):

        def put(t, row, i=i):
            for part in range(2):
                for j in range(3):
                    rows[9 * part + 3 * i + j, pl.ds(t, ROWS, stride=NT_LOCAL), :] = row[part][j]

        for partial, low, high in ((early, 0, SPLIT), (late, SPLIT, last)):

            for t in range(low, high):
                left = [[partial[t - low, 9 * part + 3 * i + j] for j in range(3)] for part in range(2)]
                put(t, row_times(left, read(held, 0)))
        put(last, [[held[0, 9 * part + 3 * i + j] for j in range(3)] for part in range(2)])
        for part in range(2):
            planes = pl.ds(9 * part + 3 * i, 3)
            copies.append(pltpu.make_async_copy(rows.at[planes], out.at[planes], sems.at[i, part]))
            copies[-1].start()
    for copy in copies:
        copy.wait()


def params():
    return pltpu.CompilerParams(vmem_limit_bytes=VMEM_LIMIT)


def field(*lead):
    return jax.ShapeDtypeStruct((*lead, 18, ROWS, LANES), jnp.float32)


def cost(flops):
    return pl.CostEstimate(flops=flops, bytes_accessed=1_000_000, transcendentals=0)


def block(*shape):
    return jax.ShapeDtypeStruct(shape, jnp.float32)


def shards(coeffs):
    count = lax.axis_size("tm")
    coeffs = coeffs.reshape(4, 8, NT_LOCAL, ROWS, LANES).swapaxes(2, 3)
    rows = coeffs.reshape(4, 8, ROWS * NT_LOCAL, LANES)
    other_rows = lax.ppermute(rows, "space", [(0, 1), (1, 0)])
    first, links, staple = pl.pallas_call(
        first_kernel,
        out_shape=(block(3, 8, ROWS, LANES), field(4, NT_LOCAL), field(NT_LOCAL)),
        in_specs=[pl.BlockSpec(memory_space=pltpu.HBM)] * 2,
        out_specs=(WHOLE, WHOLE, WHOLE),
        scratch_shapes=[
            pltpu.VMEM((4, 8, ROWS * NT_LOCAL, LANES), jnp.float32),
            pltpu.SemaphoreType.DMA,
        ],
        compiler_params=params(),
        cost_estimate=cost(1_000_000_000),
        name="first_slice",
    )(
        pltpu.with_memory_space_constraint(coeffs, pltpu.HBM),
        pltpu.with_memory_space_constraint(rows, pltpu.HBM),
    )
    ahead = lax.ppermute(first, "tm", [((i + 1) % count, i) for i in range(count)])
    links, staple = pl.pallas_call(
        local_kernel,
        out_shape=(field(4, NT_LOCAL), field(NT_LOCAL)),
        in_specs=[WHOLE] * 3,
        out_specs=(WHOLE, WHOLE),
        input_output_aliases={1: 0, 2: 1},
        compiler_params=params(),
        cost_estimate=cost(20_000_000),
        name="local_terms",
    )(rows, links, staple)
    chain_scratch = [
        pltpu.VMEM((3, 18, ROWS, LANES), jnp.float32),
        pltpu.VMEM((18, ROWS, LANES), jnp.float32),
        pltpu.VMEM((18, ROWS, LANES), jnp.float32),
    ]
    late, other_last = pl.pallas_call(
        late_chain_kernel,
        out_shape=(field(NT_LOCAL - 1 - SPLIT), field(2)),
        in_specs=[WHOLE] * 3,
        out_specs=(WHOLE, WHOLE),
        scratch_shapes=chain_scratch,
        compiler_params=params(),
        cost_estimate=cost(8_000_000),
        name="late_chain",
    )(links, staple, other_rows)
    ahead_x = pl.pallas_call(
        pick_kernel,
        out_shape=block(8, ROWS, LANES),
        in_specs=[WHOLE, WHOLE],
        out_specs=WHOLE,
        compiler_params=params(),
        name="pick",
    )(ahead, late)
    other_ahead = lax.ppermute(ahead_x, "space", [(0, 1), (1, 0)])
    early, last_terms = pl.pallas_call(
        early_chain_kernel,
        out_shape=(field(SPLIT), field()),
        in_specs=[WHOLE] * 6,
        out_specs=(WHOLE, WHOLE),
        scratch_shapes=chain_scratch + [pltpu.VMEM((3, 18, ROWS, LANES), jnp.float32)],
        compiler_params=params(),
        cost_estimate=cost(8_000_000),
        name="early_chain",
    )(links, staple, other_rows, late, other_last, ahead)
    tail, total = pl.pallas_call(
        last_slice_kernel,
        out_shape=(field(), field()),
        in_specs=[WHOLE] * 5,
        out_specs=(WHOLE, WHOLE),
        scratch_shapes=[pltpu.VMEM((18, ROWS, LANES), jnp.float32)],
        compiler_params=params(),
        cost_estimate=cost(3_000_000),
        name="last_slice",
    )(links, other_last, last_terms, other_ahead, early)
    low = 1
    while True:
        peers = LAST_PEERS if low * 4 >= count else PEERS
        received = [
            lax.ppermute(total, "tm", [(i, i ^ (low * k)) for i in range(count)]) for k in peers
        ]
        held = pltpu.VMEM((8, 18, ROWS, LANES), jnp.float32)
        if low * 4 >= count:
            break

        def level(*refs, low=low):
            level_kernel(low, *refs)

        total, tail = pl.pallas_call(
            level,
            out_shape=(field(), field()),
            in_specs=[WHOLE] * 5,
            out_specs=(WHOLE, WHOLE),
            scratch_shapes=[held],
            compiler_params=params(),
            name=f"level_{low}",
        )(total, *received, tail)
        low *= 4

    def closing(*refs, low=low):
        closing_kernel(low, *refs)

    out = pl.pallas_call(
        closing,
        out_shape=block(18, ROWS * NT_LOCAL, LANES),
        in_specs=[WHOLE] * 7,
        out_specs=pl.BlockSpec(memory_space=pltpu.HBM),
        scratch_shapes=[
            held,
            pltpu.VMEM((18, ROWS * NT_LOCAL, LANES), jnp.float32),
            pltpu.SemaphoreType.DMA((3, 2)),
        ],
        compiler_params=params(),
        name="closing",
    )(total, *received, tail, early, late)
    out = out.reshape(18, ROWS, NT_LOCAL, LANES).swapaxes(1, 2)
    return out.reshape(2, 3, 3, 1, NT_LOCAL, ROWS * LANES)


def solution(mesh):
    in_specs = (P(None, None, "space", "tm", None),)
    out_specs = P(None, None, None, "space", "tm", None)
    return jax.shard_map(shards, mesh=mesh, in_specs=in_specs, out_specs=out_specs, check_vma=False)
```

```python
import jax
import jax.numpy as jnp
from jax import lax
from jax.experimental import pallas as pl
from jax.experimental.pallas import tpu as pltpu
from jax.sharding import PartitionSpec as P

ZDIM = 32
LANES = 128
ROWS = 8
NT_LOCAL = 8
SMEAR = 0.1
SPLIT = 2
PEERS = (1, 3, 2)
LAST_PEERS = (1, 3, 2)
ROOT_THIRD = 1.0 / 3.0**0.5
VMEM_LIMIT = 48 * 1024 * 1024
WHOLE = pl.BlockSpec(memory_space=pltpu.VMEM)


def read(ref, *index):
    re = [[ref[(*index, 3 * i + j)] for j in range(3)] for i in range(3)]
    im = [[ref[(*index, 9 + 3 * i + j)] for j in range(3)] for i in range(3)]
    return re, im


def write(ref, matrix, *index):
    for part in range(2):
        for i in range(3):
            for j in range(3):
                ref[(*index, 9 * part + 3 * i + j)] = matrix[part][i][j]


def row_times(row, matrix, conj_left=False, conj_right=False):
    a, b = row
    c, d = matrix
    out_re, out_im = [], []
    for j in range(3):
        rr = a[0] * c[0][j]
        ii = b[0] * d[0][j]
        ri = a[0] * d[0][j]
        ir = b[0] * c[0][j]
        for m in (1, 2):
            rr = rr + a[m] * c[m][j]
            ii = ii + b[m] * d[m][j]
            ri = ri + a[m] * d[m][j]
            ir = ir + b[m] * c[m][j]
        out_re.append(rr + ii if conj_left != conj_right else rr - ii)
        if conj_left and conj_right:
            out_im.append(-(ri + ir))
        elif conj_left:
            out_im.append(ri - ir)
        elif conj_right:
            out_im.append(ir - ri)
        else:
            out_im.append(ri + ir)
    return out_re, out_im


def mul(left, right):
    re, im = [], []
    for i in range(3):
        r, m = row_times((left[0][i], left[1][i]), right)
        re.append(r)
        im.append(m)
    return re, im


def transposed(matrix):
    return tuple([[part[j][i] for j in range(3)] for i in range(3)] for part in matrix)


def forward_term(link, temporal, ahead):
    turned = transposed(ahead)
    re, im = [], []
    for i in range(3):
        row = row_times((link[0][i], link[1][i]), temporal)
        r, m = row_times(row, turned, conj_right=True)
        re.append(r)
        im.append(m)
    return re, im


def backward_term(link, temporal, ahead):
    turned = transposed(link)
    re, im = [], []
    for i in range(3):
        row = row_times((turned[0][i], turned[1][i]), temporal, conj_left=True)
        r, m = row_times(row, ahead)
        re.append(r)
        im.append(m)
    return re, im


def plus(left, right):
    return tuple(
        [[left[p][i][j] + right[p][i][j] for j in range(3)] for i in range(3)] for p in range(2)
    )


def mapped(f, matrix):
    return tuple([[f(part[i][j]) for j in range(3)] for i in range(3)] for part in matrix)


def lane():
    return lax.broadcasted_iota(jnp.int32, (ROWS, LANES), 1)


def from_y_above(x):
    r = pltpu.roll(x, LANES - ZDIM, 1)
    return jnp.where(lane() >= LANES - ZDIM, pltpu.roll(r, ROWS - 1, 0), r)


def from_y_below(x):
    r = pltpu.roll(x, ZDIM, 1)
    return jnp.where(lane() < ZDIM, pltpu.roll(r, 1, 0), r)


def from_z_above(x):
    edge = lane() % ZDIM == ZDIM - 1
    return jnp.where(edge, pltpu.roll(x, ZDIM - 1, 1), pltpu.roll(x, LANES - 1, 1))


def from_z_below(x):
    edge = lane() % ZDIM == 0
    return jnp.where(edge, pltpu.roll(x, LANES - ZDIM + 1, 1), pltpu.roll(x, 1, 1))


def squared(d, g01, g02, g12):
    n01 = g01[0] * g01[0] + g01[1] * g01[1]
    n02 = g02[0] * g02[0] + g02[1] * g02[1]
    n12 = g12[0] * g12[0] + g12[1] * g12[1]
    s = (d[0] * d[0] + (n01 + n02), d[1] * d[1] + (n01 + n12), d[2] * d[2] + (n02 + n12))
    k = (g01[0] * g12[0] - g01[1] * g12[1], g01[0] * g12[1] + g01[1] * g12[0])
    s02 = (k[0] - d[1] * g02[0], k[1] - d[1] * g02[1])
    s01 = (
        (g02[0] * g12[0] + g02[1] * g12[1]) - d[2] * g01[0],
        (g02[1] * g12[0] - g02[0] * g12[1]) - d[2] * g01[1],
    )
    s12 = (
        (g01[0] * g02[0] + g01[1] * g02[1]) - d[0] * g12[0],
        (g01[0] * g02[1] - g01[1] * g02[0]) - d[0] * g12[1],
    )
    det = (
        d[0] * (d[1] * d[2] - n12)
        - d[1] * n02
        - d[2] * n01
        + 2.0 * (k[0] * g02[0] + k[1] * g02[1])
    )
    return s, s01, s02, s12, det


def link_of(c):
    d2 = c[7] * (-2.0 * ROOT_THIRD)
    e = c[7] * ROOT_THIRD
    d = (e + c[2], e - c[2], d2)
    g01, g02, g12 = (c[0], -c[1]), (c[3], -c[4]), (c[5], -c[6])
    s, s01, s02, s12, det = squared(d, g01, g02, g12)
    p = (s[0] + s[1] + s[2]) * 0.125
    q = det * 0.125
    qq = q * q
    w = (p * (-1.0 / 5040.0) + 1.0 / 120.0) * p - 1.0 / 6.0
    f0r = qq * (p * (1.0 / 20160.0) - 1.0 / 720.0) + 1.0
    f0i = q * w
    f1r = q * ((p * (0.5 / 13440.0) - 0.5 / 360.0) * p + 0.5 / 24.0)
    f1i = (p * w + qq * (-1.0 / 5040.0)) * 0.5 + 0.5
    f2r = ((p * (0.25 / 40320.0) - 0.25 / 720.0) * p + 0.25 / 24.0) * p + (qq * (0.25 / 40320.0) - 0.125)
    f2i = q * (p * (-0.5 / 5040.0) + 0.25 / 120.0)
    re = [[None] * 3 for _ in range(3)]
    im = [[None] * 3 for _ in range(3)]
    for j in range(3):
        re[j][j] = f0r + (f1r * d[j] + f2r * s[j])
        im[j][j] = f0i + (f1i * d[j] + f2i * s[j])
    for j, k, g, h in ((0, 1, g01, s01), (0, 2, g02, s02), (1, 2, g12, s12)):
        rr = f1r * g[0] + f2r * h[0]
        ii = f1i * g[1] + f2i * h[1]
        ir = f1i * g[0] + f2i * h[0]
        ri = f1r * g[1] + f2r * h[1]
        re[j][k], re[k][j] = rr - ii, rr + ii
        im[j][k], im[k][j] = ir + ri, ir - ri
    return re, im


def smearing(staple, temporal):
    cr, ci = staple
    ur, ui = temporal

    def omega_re(j, k):
        t = cr[j][0] * ur[k][0] + ci[j][0] * ui[k][0]
        for m in (1, 2):
            t = t + (cr[j][m] * ur[k][m] + ci[j][m] * ui[k][m])
        return t

    def omega_im(j, k):
        t = ci[j][0] * ur[k][0] - cr[j][0] * ui[k][0]
        for m in (1, 2):
            t = t + (ci[j][m] * ur[k][m] - cr[j][m] * ui[k][m])
        return t

    half = 0.5 * SMEAR
    diag = [omega_im(j, j) for j in range(3)]
    third = (diag[0] + diag[1] + diag[2]) * (1.0 / 3.0)
    d = [(x - third) * SMEAR for x in diag]
    g = {}
    for j, k in ((0, 1), (0, 2), (1, 2)):
        g[j, k] = (
            (omega_im(j, k) + omega_im(k, j)) * half,
            (omega_re(k, j) - omega_re(j, k)) * half,
        )
    s, s01, s02, s12, q = squared(d, g[0, 1], g[0, 2], g[1, 2])
    p = (s[0] + s[1] + s[2]) * 0.5
    f1 = p * (-1.0 / 6.0) + 1.0
    f0i = q * (-1.0 / 6.0)
    re = [[None] * 3 for _ in range(3)]
    im = [[None] * 3 for _ in range(3)]
    for j in range(3):
        re[j][j] = 1.0 - 0.5 * s[j]
        im[j][j] = f0i + f1 * d[j]
    for j, k, h in ((0, 1, s01), (0, 2, s02), (1, 2, s12)):
        a = f1 * g[j, k][0]
        b = f1 * g[j, k][1]
        c = 0.5 * h[0]
        e = 0.5 * h[1]
        re[j][k], re[k][j] = -b - c, b - c
        im[j][k], im[k][j] = a - e, a + e
    return re, im


def slice_of(rows, n, t):
    return [rows[n, a, pl.ds(t, ROWS, stride=NT_LOCAL), :] for a in range(8)]


def unit():
    one = jnp.ones((ROWS, LANES), jnp.float32)
    zero = jnp.zeros((ROWS, LANES), jnp.float32)
    return (
        [[one if i == j else zero for j in range(3)] for i in range(3)],
        [[zero] * 3 for _ in range(3)],
    )


def plane_terms(spatial, temporal, ahead, above, below):
    forward = forward_term(spatial, mapped(above, temporal), ahead)
    return plus(forward, mapped(below, backward_term(spatial, temporal, ahead)))


def make_links(rows, links):
    def step(t, carry):
        for direction in range(4):
            write(links, link_of(slice_of(rows, direction, t)), direction, t)
        return carry

    lax.fori_loop(0, NT_LOCAL, step, 0)


def make_staple(links, staple):
    def step(t, carry):
        terms = plane_terms(
            read(links, 1, t), read(links, 3, t), read(links, 1, t + 1), from_y_above, from_y_below
        )
        write(staple, terms, t)
        terms = plane_terms(
            read(links, 2, t), read(links, 3, t), read(links, 2, t + 1), from_z_above, from_z_below
        )
        write(staple, plus(read(staple, t), terms), t)
        return carry

    lax.fori_loop(0, NT_LOCAL - 1, step, 0)


def first_kernel(coeffs, coeffs_by_row, first, links, staple, rows, sem):
    copy = pltpu.make_async_copy(coeffs.at[pl.ds(0, 3), :, :, 0, :], first, sem)
    copy.start()
    copy.wait()

    @pl.when(lax.axis_index("tm") == 0)
    def _():
        fetch = pltpu.make_async_copy(coeffs_by_row, rows, sem)
        fetch.start()
        fetch.wait()
        make_links(rows, links)
        make_staple(links, staple)


def links_kernel(rows, links_before, links, sent):
    del links_before
    for n, direction in enumerate((0, 3)):
        for a in range(8):
            sent[n, a] = rows[direction, a]

    @pl.when(lax.axis_index("tm") != 0)
    def _():
        make_links(rows, links)


def staple_kernel(links, staple_before, staple):
    del staple_before

    @pl.when(lax.axis_index("tm") != 0)
    def _():
        make_staple(links, staple)


def chain_steps(high, low, links, staple, rows, other_links, terms, later, put):
    def step(i, carry):
        t = high - 1 - i
        write(other_links, link_of(slice_of(rows, 1, t)), 1)
        write(other_links, link_of(slice_of(rows, 0, t)), 2)
        write(
            terms,
            plus(
                read(staple, t),
                forward_term(read(links, 0, t), read(other_links, 1), read(links, 0, t + 1)),
            ),
        )
        write(
            terms,
            plus(
                read(terms),
                backward_term(read(other_links, 2), read(other_links, 1), read(other_links, 0)),
            ),
        )
        temporal = read(links, 3, t)
        smeared = mul(smearing(read(terms), temporal), temporal)
        running = mul(smeared, read(later))
        write(later, running)
        put(t, running)
        write(other_links, read(other_links, 2), 0)
        return carry

    lax.fori_loop(0, high - low, step, 0)


def late_chain_kernel(links, staple, rows, partial, other_last, other_links, terms, later):
    last = NT_LOCAL - 1
    for n in range(2):
        write(other_last, link_of(slice_of(rows, n, last)), n)
    write(other_links, read(other_last, 0), 0)
    write(later, unit())

    def put(t, product):
        write(partial, product, t - SPLIT)

    chain_steps(last, SPLIT, links, staple, rows, other_links, terms, later, put)


def early_chain_kernel(
    links, staple, rows, late, other_last, next_rows, partial, last_terms, other_links, terms, later, ahead
):
    write(other_links, link_of(slice_of(rows, 0, SPLIT)), 0)
    write(later, read(late, 0))

    def put(t, product):
        write(partial, product, t)

    chain_steps(SPLIT, 0, links, staple, rows, other_links, terms, later, put)
    last = NT_LOCAL - 1
    for direction in range(3):
        write(ahead, link_of([next_rows[direction, a] for a in range(8)]), direction)
    temporal = read(links, 3, last)
    write(
        last_terms,
        plane_terms(read(links, 1, last), temporal, read(ahead, 1), from_y_above, from_y_below),
    )
    for term in (
        lambda: plane_terms(read(links, 2, last), temporal, read(ahead, 2), from_z_above, from_z_below),
        lambda: forward_term(read(links, 0, last), read(other_last, 1), read(ahead, 0)),
    ):
        write(last_terms, plus(read(last_terms), term()))


def pick_kernel(ahead, after, out):
    del after
    out[...] = ahead[0]


def last_slice_kernel(links, other_last, last_terms, other_next, partial, smeared_last, total, ahead):
    write(ahead, link_of([other_next[a] for a in range(8)]))
    temporal = read(links, 3, NT_LOCAL - 1)
    terms = plus(
        read(last_terms), backward_term(read(other_last, 0), read(other_last, 1), read(ahead))
    )
    write(ahead, terms)
    smeared = mul(smearing(read(ahead), temporal), temporal)
    write(smeared_last, smeared)
    write(total, mul(read(partial, 0), read(smeared_last)))


def suffixes(low, peers, own, by1, by2, by3, held):
    digit = lax.rem(lax.axis_index("tm") // low, 4)
    for k, ref in zip((0, *peers), (own, by1, by2, by3)):
        for a in range(18):
            held[k, a] = ref[a]
    third = read(held, 3 ^ digit)
    second = mul(read(held, 2 ^ digit), third)
    first = mul(read(held, 1 ^ digit), second)
    zeroth = read(held, digit)
    for k, matrix in enumerate((first, second, third, unit())):
        write(held, matrix, 4 + k)
    return zeroth, 4 + digit


def level_kernel(low, own, by1, by2, by3, tail, new_total, new_tail, held):
    zeroth, at = suffixes(low, PEERS, own, by1, by2, by3, held)
    write(new_total, mul(zeroth, read(held, 4)))
    write(new_tail, mul(read(tail), read(held, at)))


def closing_kernel(low, own, by1, by2, by3, tail, early, late, out, held, rows, sems):
    _, at = suffixes(low, LAST_PEERS, own, by1, by2, by3, held)
    write(held, mul(read(tail), read(held, at)), 0)
    last = NT_LOCAL - 1
    copies = []
    for i in range(3):

        def put(t, row, i=i):
            for part in range(2):
                for j in range(3):
                    rows[9 * part + 3 * i + j, pl.ds(t, ROWS, stride=NT_LOCAL), :] = row[part][j]

        for partial, low, high in ((early, 0, SPLIT), (late, SPLIT, last)):

            for t in range(low, high):
                left = [[partial[t - low, 9 * part + 3 * i + j] for j in range(3)] for part in range(2)]
                put(t, row_times(left, read(held, 0)))
        put(last, [[held[0, 9 * part + 3 * i + j] for j in range(3)] for part in range(2)])
        for part in range(2):
            planes = pl.ds(9 * part + 3 * i, 3)
            copies.append(pltpu.make_async_copy(rows.at[planes], out.at[planes], sems.at[i, part]))
            copies[-1].start()
    for copy in copies:
        copy.wait()


def params():
    return pltpu.CompilerParams(vmem_limit_bytes=VMEM_LIMIT)


def field(*lead):
    return jax.ShapeDtypeStruct((*lead, 18, ROWS, LANES), jnp.float32)


def cost(flops):
    return pl.CostEstimate(flops=flops, bytes_accessed=1_000_000, transcendentals=0)


def block(*shape):
    return jax.ShapeDtypeStruct(shape, jnp.float32)


def shards(coeffs):
    count = lax.axis_size("tm")
    coeffs = coeffs.reshape(4, 8, NT_LOCAL, ROWS, LANES).swapaxes(2, 3)
    rows = coeffs.reshape(4, 8, ROWS * NT_LOCAL, LANES)
    first, links, staple = pl.pallas_call(
        first_kernel,
        out_shape=(block(3, 8, ROWS, LANES), field(4, NT_LOCAL), field(NT_LOCAL)),
        in_specs=[pl.BlockSpec(memory_space=pltpu.HBM)] * 2,
        out_specs=(WHOLE, WHOLE, WHOLE),
        scratch_shapes=[
            pltpu.VMEM((4, 8, ROWS * NT_LOCAL, LANES), jnp.float32),
            pltpu.SemaphoreType.DMA,
        ],
        compiler_params=params(),
        cost_estimate=cost(1_000_000_000),
        name="first_slice",
    )(
        pltpu.with_memory_space_constraint(coeffs, pltpu.HBM),
        pltpu.with_memory_space_constraint(rows, pltpu.HBM),
    )
    ahead = lax.ppermute(first, "tm", [((i + 1) % count, i) for i in range(count)])
    links, sent = pl.pallas_call(
        links_kernel,
        out_shape=(field(4, NT_LOCAL), block(2, 8, ROWS * NT_LOCAL, LANES)),
        in_specs=[WHOLE] * 2,
        out_specs=(WHOLE, WHOLE),
        input_output_aliases={1: 0},
        compiler_params=params(),
        cost_estimate=cost(10_000_000),
        name="links",
    )(rows, links)
    other_rows = lax.ppermute(sent, "space", [(0, 1), (1, 0)])
    staple = pl.pallas_call(
        staple_kernel,
        out_shape=field(NT_LOCAL),
        in_specs=[WHOLE] * 2,
        out_specs=WHOLE,
        input_output_aliases={1: 0},
        compiler_params=params(),
        cost_estimate=cost(20_000_000_000),
        name="staple",
    )(links, staple)
    chain_scratch = [
        pltpu.VMEM((3, 18, ROWS, LANES), jnp.float32),
        pltpu.VMEM((18, ROWS, LANES), jnp.float32),
        pltpu.VMEM((18, ROWS, LANES), jnp.float32),
    ]
    late, other_last = pl.pallas_call(
        late_chain_kernel,
        out_shape=(field(NT_LOCAL - 1 - SPLIT), field(2)),
        in_specs=[WHOLE] * 3,
        out_specs=(WHOLE, WHOLE),
        scratch_shapes=chain_scratch,
        compiler_params=params(),
        cost_estimate=cost(8_000_000),
        name="late_chain",
    )(links, staple, other_rows)
    ahead_x = pl.pallas_call(
        pick_kernel,
        out_shape=block(8, ROWS, LANES),
        in_specs=[WHOLE, WHOLE],
        out_specs=WHOLE,
        compiler_params=params(),
        name="pick",
    )(ahead, late)
    other_ahead = lax.ppermute(ahead_x, "space", [(0, 1), (1, 0)])
    early, last_terms = pl.pallas_call(
        early_chain_kernel,
        out_shape=(field(SPLIT), field()),
        in_specs=[WHOLE] * 6,
        out_specs=(WHOLE, WHOLE),
        scratch_shapes=chain_scratch + [pltpu.VMEM((3, 18, ROWS, LANES), jnp.float32)],
        compiler_params=params(),
        cost_estimate=cost(8_000_000),
        name="early_chain",
    )(links, staple, other_rows, late, other_last, ahead)
    tail, total = pl.pallas_call(
        last_slice_kernel,
        out_shape=(field(), field()),
        in_specs=[WHOLE] * 5,
        out_specs=(WHOLE, WHOLE),
        scratch_shapes=[pltpu.VMEM((18, ROWS, LANES), jnp.float32)],
        compiler_params=params(),
        cost_estimate=cost(3_000_000),
        name="last_slice",
    )(links, other_last, last_terms, other_ahead, early)
    low = 1
    while True:
        peers = LAST_PEERS if low * 4 >= count else PEERS
        received = [
            lax.ppermute(total, "tm", [(i, i ^ (low * k)) for i in range(count)]) for k in peers
        ]
        held = pltpu.VMEM((8, 18, ROWS, LANES), jnp.float32)
        if low * 4 >= count:
            break

        def level(*refs, low=low):
            level_kernel(low, *refs)

        total, tail = pl.pallas_call(
            level,
            out_shape=(field(), field()),
            in_specs=[WHOLE] * 5,
            out_specs=(WHOLE, WHOLE),
            scratch_shapes=[held],
            compiler_params=params(),
            name=f"level_{low}",
        )(total, *received, tail)
        low *= 4

    def closing(*refs, low=low):
        closing_kernel(low, *refs)

    out = pl.pallas_call(
        closing,
        out_shape=block(18, ROWS * NT_LOCAL, LANES),
        in_specs=[WHOLE] * 7,
        out_specs=pl.BlockSpec(memory_space=pltpu.HBM),
        scratch_shapes=[
            held,
            pltpu.VMEM((18, ROWS * NT_LOCAL, LANES), jnp.float32),
            pltpu.SemaphoreType.DMA((3, 2)),
        ],
        compiler_params=params(),
        name="closing",
    )(total, *received, tail, early, late)
    out = out.reshape(18, ROWS, NT_LOCAL, LANES).swapaxes(1, 2)
    return out.reshape(2, 3, 3, 1, NT_LOCAL, ROWS * LANES)


def solution(mesh):
    in_specs = (P(None, None, "space", "tm", None),)
    out_specs = P(None, None, None, "space", "tm", None)
    return jax.shard_map(shards, mesh=mesh, in_specs=in_specs, out_specs=out_specs, check_vma=False)
```

```python
import jax
import jax.numpy as jnp
from jax import lax
from jax.experimental import pallas as pl
from jax.experimental.pallas import tpu as pltpu
from jax.sharding import PartitionSpec as P

ZDIM = 32
LANES = 128
ROWS = 8
NT_LOCAL = 8
SMEAR = 0.1
SPLIT = 2
PEERS = (1, 3, 2)
LAST_PEERS = (1, 3, 2)
ROOT_THIRD = 1.0 / 3.0**0.5
VMEM_LIMIT = 48 * 1024 * 1024
WHOLE = pl.BlockSpec(memory_space=pltpu.VMEM)


def read(ref, *index):
    re = [[ref[(*index, 3 * i + j)] for j in range(3)] for i in range(3)]
    im = [[ref[(*index, 9 + 3 * i + j)] for j in range(3)] for i in range(3)]
    return re, im


def write(ref, matrix, *index):
    for part in range(2):
        for i in range(3):
            for j in range(3):
                ref[(*index, 9 * part + 3 * i + j)] = matrix[part][i][j]


def row_times(row, matrix, conj_left=False, conj_right=False):
    a, b = row
    c, d = matrix
    out_re, out_im = [], []
    for j in range(3):
        rr = a[0] * c[0][j]
        ii = b[0] * d[0][j]
        ri = a[0] * d[0][j]
        ir = b[0] * c[0][j]
        for m in (1, 2):
            rr = rr + a[m] * c[m][j]
            ii = ii + b[m] * d[m][j]
            ri = ri + a[m] * d[m][j]
            ir = ir + b[m] * c[m][j]
        out_re.append(rr + ii if conj_left != conj_right else rr - ii)
        if conj_left and conj_right:
            out_im.append(-(ri + ir))
        elif conj_left:
            out_im.append(ri - ir)
        elif conj_right:
            out_im.append(ir - ri)
        else:
            out_im.append(ri + ir)
    return out_re, out_im


def mul(left, right):
    re, im = [], []
    for i in range(3):
        r, m = row_times((left[0][i], left[1][i]), right)
        re.append(r)
        im.append(m)
    return re, im


def transposed(matrix):
    return tuple([[part[j][i] for j in range(3)] for i in range(3)] for part in matrix)


def forward_term(link, temporal, ahead):
    turned = transposed(ahead)
    re, im = [], []
    for i in range(3):
        row = row_times((link[0][i], link[1][i]), temporal)
        r, m = row_times(row, turned, conj_right=True)
        re.append(r)
        im.append(m)
    return re, im


def backward_term(link, temporal, ahead):
    turned = transposed(link)
    re, im = [], []
    for i in range(3):
        row = row_times((turned[0][i], turned[1][i]), temporal, conj_left=True)
        r, m = row_times(row, ahead)
        re.append(r)
        im.append(m)
    return re, im


def plus(left, right):
    return tuple(
        [[left[p][i][j] + right[p][i][j] for j in range(3)] for i in range(3)] for p in range(2)
    )


def mapped(f, matrix):
    return tuple([[f(part[i][j]) for j in range(3)] for i in range(3)] for part in matrix)


def lane():
    return lax.broadcasted_iota(jnp.int32, (ROWS, LANES), 1)


def from_y_above(x):
    r = pltpu.roll(x, LANES - ZDIM, 1)
    return jnp.where(lane() >= LANES - ZDIM, pltpu.roll(r, ROWS - 1, 0), r)


def from_y_below(x):
    r = pltpu.roll(x, ZDIM, 1)
    return jnp.where(lane() < ZDIM, pltpu.roll(r, 1, 0), r)


def from_z_above(x):
    edge = lane() % ZDIM == ZDIM - 1
    return jnp.where(edge, pltpu.roll(x, ZDIM - 1, 1), pltpu.roll(x, LANES - 1, 1))


def from_z_below(x):
    edge = lane() % ZDIM == 0
    return jnp.where(edge, pltpu.roll(x, LANES - ZDIM + 1, 1), pltpu.roll(x, 1, 1))


def squared(d, g01, g02, g12):
    n01 = g01[0] * g01[0] + g01[1] * g01[1]
    n02 = g02[0] * g02[0] + g02[1] * g02[1]
    n12 = g12[0] * g12[0] + g12[1] * g12[1]
    s = (d[0] * d[0] + (n01 + n02), d[1] * d[1] + (n01 + n12), d[2] * d[2] + (n02 + n12))
    k = (g01[0] * g12[0] - g01[1] * g12[1], g01[0] * g12[1] + g01[1] * g12[0])
    s02 = (k[0] - d[1] * g02[0], k[1] - d[1] * g02[1])
    s01 = (
        (g02[0] * g12[0] + g02[1] * g12[1]) - d[2] * g01[0],
        (g02[1] * g12[0] - g02[0] * g12[1]) - d[2] * g01[1],
    )
    s12 = (
        (g01[0] * g02[0] + g01[1] * g02[1]) - d[0] * g12[0],
        (g01[0] * g02[1] - g01[1] * g02[0]) - d[0] * g12[1],
    )
    det = (
        d[0] * (d[1] * d[2] - n12)
        - d[1] * n02
        - d[2] * n01
        + 2.0 * (k[0] * g02[0] + k[1] * g02[1])
    )
    return s, s01, s02, s12, det


def link_of(c):
    d2 = c[7] * (-2.0 * ROOT_THIRD)
    e = c[7] * ROOT_THIRD
    d = (e + c[2], e - c[2], d2)
    g01, g02, g12 = (c[0], -c[1]), (c[3], -c[4]), (c[5], -c[6])
    s, s01, s02, s12, det = squared(d, g01, g02, g12)
    p = (s[0] + s[1] + s[2]) * 0.125
    q = det * 0.125
    qq = q * q
    w = (p * (-1.0 / 5040.0) + 1.0 / 120.0) * p - 1.0 / 6.0
    f0r = qq * (p * (1.0 / 20160.0) - 1.0 / 720.0) + 1.0
    f0i = q * w
    f1r = q * ((p * (0.5 / 13440.0) - 0.5 / 360.0) * p + 0.5 / 24.0)
    f1i = (p * w + qq * (-1.0 / 5040.0)) * 0.5 + 0.5
    f2r = ((p * (0.25 / 40320.0) - 0.25 / 720.0) * p + 0.25 / 24.0) * p + (qq * (0.25 / 40320.0) - 0.125)
    f2i = q * (p * (-0.5 / 5040.0) + 0.25 / 120.0)
    re = [[None] * 3 for _ in range(3)]
    im = [[None] * 3 for _ in range(3)]
    for j in range(3):
        re[j][j] = f0r + (f1r * d[j] + f2r * s[j])
        im[j][j] = f0i + (f1i * d[j] + f2i * s[j])
    for j, k, g, h in ((0, 1, g01, s01), (0, 2, g02, s02), (1, 2, g12, s12)):
        rr = f1r * g[0] + f2r * h[0]
        ii = f1i * g[1] + f2i * h[1]
        ir = f1i * g[0] + f2i * h[0]
        ri = f1r * g[1] + f2r * h[1]
        re[j][k], re[k][j] = rr - ii, rr + ii
        im[j][k], im[k][j] = ir + ri, ir - ri
    return re, im


def smearing(staple, temporal):
    cr, ci = staple
    ur, ui = temporal

    def omega_re(j, k):
        t = cr[j][0] * ur[k][0] + ci[j][0] * ui[k][0]
        for m in (1, 2):
            t = t + (cr[j][m] * ur[k][m] + ci[j][m] * ui[k][m])
        return t

    def omega_im(j, k):
        t = ci[j][0] * ur[k][0] - cr[j][0] * ui[k][0]
        for m in (1, 2):
            t = t + (ci[j][m] * ur[k][m] - cr[j][m] * ui[k][m])
        return t

    half = 0.5 * SMEAR
    diag = [omega_im(j, j) for j in range(3)]
    third = (diag[0] + diag[1] + diag[2]) * (1.0 / 3.0)
    d = [(x - third) * SMEAR for x in diag]
    g = {}
    for j, k in ((0, 1), (0, 2), (1, 2)):
        g[j, k] = (
            (omega_im(j, k) + omega_im(k, j)) * half,
            (omega_re(k, j) - omega_re(j, k)) * half,
        )
    s, s01, s02, s12, q = squared(d, g[0, 1], g[0, 2], g[1, 2])
    p = (s[0] + s[1] + s[2]) * 0.5
    f1 = p * (-1.0 / 6.0) + 1.0
    f0i = q * (-1.0 / 6.0)
    re = [[None] * 3 for _ in range(3)]
    im = [[None] * 3 for _ in range(3)]
    for j in range(3):
        re[j][j] = 1.0 - 0.5 * s[j]
        im[j][j] = f0i + f1 * d[j]
    for j, k, h in ((0, 1, s01), (0, 2, s02), (1, 2, s12)):
        a = f1 * g[j, k][0]
        b = f1 * g[j, k][1]
        c = 0.5 * h[0]
        e = 0.5 * h[1]
        re[j][k], re[k][j] = -b - c, b - c
        im[j][k], im[k][j] = a - e, a + e
    return re, im


def slice_of(rows, n, t):
    return [rows[n, a, pl.ds(t, ROWS, stride=NT_LOCAL), :] for a in range(8)]


def unit():
    one = jnp.ones((ROWS, LANES), jnp.float32)
    zero = jnp.zeros((ROWS, LANES), jnp.float32)
    return (
        [[one if i == j else zero for j in range(3)] for i in range(3)],
        [[zero] * 3 for _ in range(3)],
    )


def plane_terms(spatial, temporal, ahead, above, below):
    forward = forward_term(spatial, mapped(above, temporal), ahead)
    return plus(forward, mapped(below, backward_term(spatial, temporal, ahead)))


def make_links(rows, links):
    def step(t, carry):
        for direction in range(4):
            write(links, link_of(slice_of(rows, direction, t)), direction, t)
        return carry

    lax.fori_loop(0, NT_LOCAL, step, 0)


def make_staple(links, staple):
    def step(t, carry):
        terms = plane_terms(
            read(links, 1, t), read(links, 3, t), read(links, 1, t + 1), from_y_above, from_y_below
        )
        write(staple, terms, t)
        terms = plane_terms(
            read(links, 2, t), read(links, 3, t), read(links, 2, t + 1), from_z_above, from_z_below
        )
        write(staple, plus(read(staple, t), terms), t)
        return carry

    lax.fori_loop(0, NT_LOCAL - 1, step, 0)


def first_kernel(coeffs, coeffs_by_row, first, links, staple, rows, sem):
    copy = pltpu.make_async_copy(coeffs.at[pl.ds(0, 3), :, :, 0, :], first, sem)
    copy.start()
    copy.wait()

    @pl.when(lax.rem(lax.axis_index("tm"), 16) == 0)
    def _():
        fetch = pltpu.make_async_copy(coeffs_by_row, rows, sem)
        fetch.start()
        fetch.wait()
        make_links(rows, links)

    @pl.when(lax.axis_index("tm") == 0)
    def _():
        make_staple(links, staple)


def links_kernel(rows, links_before, links, sent):
    del links_before
    for n, direction in enumerate((0, 3)):
        for a in range(8):
            sent[n, a] = rows[direction, a]

    @pl.when(lax.rem(lax.axis_index("tm"), 16) != 0)
    def _():
        make_links(rows, links)


def staple_kernel(links, staple_before, staple):
    del staple_before

    @pl.when(lax.axis_index("tm") != 0)
    def _():
        make_staple(links, staple)


def chain_steps(high, low, links, staple, rows, other_links, terms, later, put):
    def step(i, carry):
        t = high - 1 - i
        write(other_links, link_of(slice_of(rows, 1, t)), 1)
        write(other_links, link_of(slice_of(rows, 0, t)), 2)
        write(
            terms,
            plus(
                read(staple, t),
                forward_term(read(links, 0, t), read(other_links, 1), read(links, 0, t + 1)),
            ),
        )
        write(
            terms,
            plus(
                read(terms),
                backward_term(read(other_links, 2), read(other_links, 1), read(other_links, 0)),
            ),
        )
        temporal = read(links, 3, t)
        smeared = mul(smearing(read(terms), temporal), temporal)
        running = mul(smeared, read(later))
        write(later, running)
        put(t, running)
        write(other_links, read(other_links, 2), 0)
        return carry

    lax.fori_loop(0, high - low, step, 0)


def late_chain_kernel(links, staple, rows, partial, other_last, other_links, terms, later):
    last = NT_LOCAL - 1
    for n in range(2):
        write(other_last, link_of(slice_of(rows, n, last)), n)
    write(other_links, read(other_last, 0), 0)
    write(later, unit())

    def put(t, product):
        write(partial, product, t - SPLIT)

    chain_steps(last, SPLIT, links, staple, rows, other_links, terms, later, put)


def early_chain_kernel(
    links, staple, rows, late, other_last, next_rows, partial, last_terms, other_links, terms, later, ahead
):
    write(other_links, link_of(slice_of(rows, 0, SPLIT)), 0)
    write(later, read(late, 0))

    def put(t, product):
        write(partial, product, t)

    chain_steps(SPLIT, 0, links, staple, rows, other_links, terms, later, put)
    last = NT_LOCAL - 1
    for direction in range(3):
        write(ahead, link_of([next_rows[direction, a] for a in range(8)]), direction)
    temporal = read(links, 3, last)
    write(
        last_terms,
        plane_terms(read(links, 1, last), temporal, read(ahead, 1), from_y_above, from_y_below),
    )
    for term in (
        lambda: plane_terms(read(links, 2, last), temporal, read(ahead, 2), from_z_above, from_z_below),
        lambda: forward_term(read(links, 0, last), read(other_last, 1), read(ahead, 0)),
    ):
        write(last_terms, plus(read(last_terms), term()))


def pick_kernel(ahead, after, out):
    del after
    out[...] = ahead[0]


def last_slice_kernel(links, other_last, last_terms, other_next, partial, smeared_last, total, ahead):
    write(ahead, link_of([other_next[a] for a in range(8)]))
    temporal = read(links, 3, NT_LOCAL - 1)
    terms = plus(
        read(last_terms), backward_term(read(other_last, 0), read(other_last, 1), read(ahead))
    )
    write(ahead, terms)
    smeared = mul(smearing(read(ahead), temporal), temporal)
    write(smeared_last, smeared)
    write(total, mul(read(partial, 0), read(smeared_last)))


def suffixes(low, peers, own, by1, by2, by3, held):
    digit = lax.rem(lax.axis_index("tm") // low, 4)
    for k, ref in zip((0, *peers), (own, by1, by2, by3)):
        for a in range(18):
            held[k, a] = ref[a]
    third = read(held, 3 ^ digit)
    second = mul(read(held, 2 ^ digit), third)
    first = mul(read(held, 1 ^ digit), second)
    zeroth = read(held, digit)
    for k, matrix in enumerate((first, second, third, unit())):
        write(held, matrix, 4 + k)
    return zeroth, 4 + digit


def level_kernel(low, own, by1, by2, by3, new_total, suffix, held):
    zeroth, at = suffixes(low, PEERS, own, by1, by2, by3, held)
    write(new_total, mul(zeroth, read(held, 4)))
    write(suffix, read(held, at))


def tail_kernel(tail, suffix, new_tail):
    write(new_tail, mul(read(tail), read(suffix)))


def closing_kernel(low, own, by1, by2, by3, tail, early, late, out, held, rows, sems):
    _, at = suffixes(low, LAST_PEERS, own, by1, by2, by3, held)
    write(held, mul(read(tail), read(held, at)), 0)
    last = NT_LOCAL - 1
    copies = []
    for i in range(3):

        def put(t, row, i=i):
            for part in range(2):
                for j in range(3):
                    rows[9 * part + 3 * i + j, pl.ds(t, ROWS, stride=NT_LOCAL), :] = row[part][j]

        for partial, low, high in ((early, 0, SPLIT), (late, SPLIT, last)):

            for t in range(low, high):
                left = [[partial[t - low, 9 * part + 3 * i + j] for j in range(3)] for part in range(2)]
                put(t, row_times(left, read(held, 0)))
        put(last, [[held[0, 9 * part + 3 * i + j] for j in range(3)] for part in range(2)])
        for part in range(2):
            planes = pl.ds(9 * part + 3 * i, 3)
            copies.append(pltpu.make_async_copy(rows.at[planes], out.at[planes], sems.at[i, part]))
            copies[-1].start()
    for copy in copies:
        copy.wait()


def params():
    return pltpu.CompilerParams(vmem_limit_bytes=VMEM_LIMIT)


def field(*lead):
    return jax.ShapeDtypeStruct((*lead, 18, ROWS, LANES), jnp.float32)


def cost(flops):
    return pl.CostEstimate(flops=flops, bytes_accessed=1_000_000, transcendentals=0)


def block(*shape):
    return jax.ShapeDtypeStruct(shape, jnp.float32)


def shards(coeffs):
    count = lax.axis_size("tm")
    coeffs = coeffs.reshape(4, 8, NT_LOCAL, ROWS, LANES).swapaxes(2, 3)
    rows = coeffs.reshape(4, 8, ROWS * NT_LOCAL, LANES)
    first, links, staple = pl.pallas_call(
        first_kernel,
        out_shape=(block(3, 8, ROWS, LANES), field(4, NT_LOCAL), field(NT_LOCAL)),
        in_specs=[pl.BlockSpec(memory_space=pltpu.HBM)] * 2,
        out_specs=(WHOLE, WHOLE, WHOLE),
        scratch_shapes=[
            pltpu.VMEM((4, 8, ROWS * NT_LOCAL, LANES), jnp.float32),
            pltpu.SemaphoreType.DMA,
        ],
        compiler_params=params(),
        cost_estimate=cost(1_000_000_000),
        name="first_slice",
    )(
        pltpu.with_memory_space_constraint(coeffs, pltpu.HBM),
        pltpu.with_memory_space_constraint(rows, pltpu.HBM),
    )
    ahead = lax.ppermute(first, "tm", [((i + 1) % count, i) for i in range(count)])
    links, sent = pl.pallas_call(
        links_kernel,
        out_shape=(field(4, NT_LOCAL), block(2, 8, ROWS * NT_LOCAL, LANES)),
        in_specs=[WHOLE] * 2,
        out_specs=(WHOLE, WHOLE),
        input_output_aliases={1: 0},
        compiler_params=params(),
        cost_estimate=cost(10_000_000),
        name="links",
    )(rows, links)
    other_rows = lax.ppermute(sent, "space", [(0, 1), (1, 0)])
    staple = pl.pallas_call(
        staple_kernel,
        out_shape=field(NT_LOCAL),
        in_specs=[WHOLE] * 2,
        out_specs=WHOLE,
        input_output_aliases={1: 0},
        compiler_params=params(),
        cost_estimate=cost(20_000_000_000),
        name="staple",
    )(links, staple)
    chain_scratch = [
        pltpu.VMEM((3, 18, ROWS, LANES), jnp.float32),
        pltpu.VMEM((18, ROWS, LANES), jnp.float32),
        pltpu.VMEM((18, ROWS, LANES), jnp.float32),
    ]
    late, other_last = pl.pallas_call(
        late_chain_kernel,
        out_shape=(field(NT_LOCAL - 1 - SPLIT), field(2)),
        in_specs=[WHOLE] * 3,
        out_specs=(WHOLE, WHOLE),
        scratch_shapes=chain_scratch,
        compiler_params=params(),
        cost_estimate=cost(8_000_000),
        name="late_chain",
    )(links, staple, other_rows)
    ahead_x = pl.pallas_call(
        pick_kernel,
        out_shape=block(8, ROWS, LANES),
        in_specs=[WHOLE, WHOLE],
        out_specs=WHOLE,
        compiler_params=params(),
        name="pick",
    )(ahead, late)
    other_ahead = lax.ppermute(ahead_x, "space", [(0, 1), (1, 0)])
    early, last_terms = pl.pallas_call(
        early_chain_kernel,
        out_shape=(field(SPLIT), field()),
        in_specs=[WHOLE] * 6,
        out_specs=(WHOLE, WHOLE),
        scratch_shapes=chain_scratch + [pltpu.VMEM((3, 18, ROWS, LANES), jnp.float32)],
        compiler_params=params(),
        cost_estimate=cost(8_000_000),
        name="early_chain",
    )(links, staple, other_rows, late, other_last, ahead)
    tail, total = pl.pallas_call(
        last_slice_kernel,
        out_shape=(field(), field()),
        in_specs=[WHOLE] * 5,
        out_specs=(WHOLE, WHOLE),
        scratch_shapes=[pltpu.VMEM((18, ROWS, LANES), jnp.float32)],
        compiler_params=params(),
        cost_estimate=cost(3_000_000),
        name="last_slice",
    )(links, other_last, last_terms, other_ahead, early)
    low = 1
    while True:
        peers = LAST_PEERS if low * 4 >= count else PEERS
        received = [
            lax.ppermute(total, "tm", [(i, i ^ (low * k)) for i in range(count)]) for k in peers
        ]
        held = pltpu.VMEM((8, 18, ROWS, LANES), jnp.float32)
        if low * 4 >= count:
            break

        def level(*refs, low=low):
            level_kernel(low, *refs)

        total, suffix = pl.pallas_call(
            level,
            out_shape=(field(), field()),
            in_specs=[WHOLE] * 4,
            out_specs=(WHOLE, WHOLE),
            scratch_shapes=[held],
            compiler_params=params(),
            name=f"level_{low}",
        )(total, *received)
        tail = pl.pallas_call(
            tail_kernel,
            out_shape=field(),
            in_specs=[WHOLE] * 2,
            out_specs=WHOLE,
            compiler_params=params(),
            name=f"tail_{low}",
        )(tail, suffix)
        low *= 4

    def closing(*refs, low=low):
        closing_kernel(low, *refs)

    out = pl.pallas_call(
        closing,
        out_shape=block(18, ROWS * NT_LOCAL, LANES),
        in_specs=[WHOLE] * 7,
        out_specs=pl.BlockSpec(memory_space=pltpu.HBM),
        scratch_shapes=[
            held,
            pltpu.VMEM((18, ROWS * NT_LOCAL, LANES), jnp.float32),
            pltpu.SemaphoreType.DMA((3, 2)),
        ],
        compiler_params=params(),
        name="closing",
    )(total, *received, tail, early, late)
    out = out.reshape(18, ROWS, NT_LOCAL, LANES).swapaxes(1, 2)
    return out.reshape(2, 3, 3, 1, NT_LOCAL, ROWS * LANES)


def solution(mesh):
    in_specs = (P(None, None, "space", "tm", None),)
    out_specs = P(None, None, None, "space", "tm", None)
    return jax.shard_map(shards, mesh=mesh, in_specs=in_specs, out_specs=out_specs, check_vma=False)
```

```python
import jax
import jax.numpy as jnp
from jax import lax
from jax.experimental import pallas as pl
from jax.experimental.pallas import tpu as pltpu
from jax.sharding import PartitionSpec as P

ZDIM = 32
LANES = 128
ROWS = 8
NT_LOCAL = 8
SMEAR = 0.1
SPLIT = 2
PEERS = (1, 3, 2)
LAST_PEERS = (1, 3, 2)
ROOT_THIRD = 1.0 / 3.0**0.5
VMEM_LIMIT = 48 * 1024 * 1024
WHOLE = pl.BlockSpec(memory_space=pltpu.VMEM)


def read(ref, *index):
    re = [[ref[(*index, 3 * i + j)] for j in range(3)] for i in range(3)]
    im = [[ref[(*index, 9 + 3 * i + j)] for j in range(3)] for i in range(3)]
    return re, im


def write(ref, matrix, *index):
    for part in range(2):
        for i in range(3):
            for j in range(3):
                ref[(*index, 9 * part + 3 * i + j)] = matrix[part][i][j]


def row_times(row, matrix, conj_left=False, conj_right=False):
    a, b = row
    c, d = matrix
    out_re, out_im = [], []
    for j in range(3):
        rr = a[0] * c[0][j]
        ii = b[0] * d[0][j]
        ri = a[0] * d[0][j]
        ir = b[0] * c[0][j]
        for m in (1, 2):
            rr = rr + a[m] * c[m][j]
            ii = ii + b[m] * d[m][j]
            ri = ri + a[m] * d[m][j]
            ir = ir + b[m] * c[m][j]
        out_re.append(rr + ii if conj_left != conj_right else rr - ii)
        if conj_left and conj_right:
            out_im.append(-(ri + ir))
        elif conj_left:
            out_im.append(ri - ir)
        elif conj_right:
            out_im.append(ir - ri)
        else:
            out_im.append(ri + ir)
    return out_re, out_im


def mul(left, right):
    re, im = [], []
    for i in range(3):
        r, m = row_times((left[0][i], left[1][i]), right)
        re.append(r)
        im.append(m)
    return re, im


def transposed(matrix):
    return tuple([[part[j][i] for j in range(3)] for i in range(3)] for part in matrix)


def forward_term(link, temporal, ahead):
    turned = transposed(ahead)
    re, im = [], []
    for i in range(3):
        row = row_times((link[0][i], link[1][i]), temporal)
        r, m = row_times(row, turned, conj_right=True)
        re.append(r)
        im.append(m)
    return re, im


def backward_term(link, temporal, ahead):
    turned = transposed(link)
    re, im = [], []
    for i in range(3):
        row = row_times((turned[0][i], turned[1][i]), temporal, conj_left=True)
        r, m = row_times(row, ahead)
        re.append(r)
        im.append(m)
    return re, im


def plus(left, right):
    return tuple(
        [[left[p][i][j] + right[p][i][j] for j in range(3)] for i in range(3)] for p in range(2)
    )


def mapped(f, matrix):
    return tuple([[f(part[i][j]) for j in range(3)] for i in range(3)] for part in matrix)


def lane():
    return lax.broadcasted_iota(jnp.int32, (ROWS, LANES), 1)


def from_y_above(x):
    r = pltpu.roll(x, LANES - ZDIM, 1)
    return jnp.where(lane() >= LANES - ZDIM, pltpu.roll(r, ROWS - 1, 0), r)


def from_y_below(x):
    r = pltpu.roll(x, ZDIM, 1)
    return jnp.where(lane() < ZDIM, pltpu.roll(r, 1, 0), r)


def from_z_above(x):
    edge = lane() % ZDIM == ZDIM - 1
    return jnp.where(edge, pltpu.roll(x, ZDIM - 1, 1), pltpu.roll(x, LANES - 1, 1))


def from_z_below(x):
    edge = lane() % ZDIM == 0
    return jnp.where(edge, pltpu.roll(x, LANES - ZDIM + 1, 1), pltpu.roll(x, 1, 1))


def squared(d, g01, g02, g12):
    n01 = g01[0] * g01[0] + g01[1] * g01[1]
    n02 = g02[0] * g02[0] + g02[1] * g02[1]
    n12 = g12[0] * g12[0] + g12[1] * g12[1]
    s = (d[0] * d[0] + (n01 + n02), d[1] * d[1] + (n01 + n12), d[2] * d[2] + (n02 + n12))
    k = (g01[0] * g12[0] - g01[1] * g12[1], g01[0] * g12[1] + g01[1] * g12[0])
    s02 = (k[0] - d[1] * g02[0], k[1] - d[1] * g02[1])
    s01 = (
        (g02[0] * g12[0] + g02[1] * g12[1]) - d[2] * g01[0],
        (g02[1] * g12[0] - g02[0] * g12[1]) - d[2] * g01[1],
    )
    s12 = (
        (g01[0] * g02[0] + g01[1] * g02[1]) - d[0] * g12[0],
        (g01[0] * g02[1] - g01[1] * g02[0]) - d[0] * g12[1],
    )
    det = (
        d[0] * (d[1] * d[2] - n12)
        - d[1] * n02
        - d[2] * n01
        + 2.0 * (k[0] * g02[0] + k[1] * g02[1])
    )
    return s, s01, s02, s12, det


def link_of(c):
    d2 = c[7] * (-2.0 * ROOT_THIRD)
    e = c[7] * ROOT_THIRD
    d = (e + c[2], e - c[2], d2)
    g01, g02, g12 = (c[0], -c[1]), (c[3], -c[4]), (c[5], -c[6])
    s, s01, s02, s12, det = squared(d, g01, g02, g12)
    p = (s[0] + s[1] + s[2]) * 0.125
    q = det * 0.125
    qq = q * q
    w = (p * (-1.0 / 5040.0) + 1.0 / 120.0) * p - 1.0 / 6.0
    f0r = qq * (p * (1.0 / 20160.0) - 1.0 / 720.0) + 1.0
    f0i = q * w
    f1r = q * ((p * (0.5 / 13440.0) - 0.5 / 360.0) * p + 0.5 / 24.0)
    f1i = (p * w + qq * (-1.0 / 5040.0)) * 0.5 + 0.5
    f2r = ((p * (0.25 / 40320.0) - 0.25 / 720.0) * p + 0.25 / 24.0) * p + (qq * (0.25 / 40320.0) - 0.125)
    f2i = q * (p * (-0.5 / 5040.0) + 0.25 / 120.0)
    re = [[None] * 3 for _ in range(3)]
    im = [[None] * 3 for _ in range(3)]
    for j in range(3):
        re[j][j] = f0r + (f1r * d[j] + f2r * s[j])
        im[j][j] = f0i + (f1i * d[j] + f2i * s[j])
    for j, k, g, h in ((0, 1, g01, s01), (0, 2, g02, s02), (1, 2, g12, s12)):
        rr = f1r * g[0] + f2r * h[0]
        ii = f1i * g[1] + f2i * h[1]
        ir = f1i * g[0] + f2i * h[0]
        ri = f1r * g[1] + f2r * h[1]
        re[j][k], re[k][j] = rr - ii, rr + ii
        im[j][k], im[k][j] = ir + ri, ir - ri
    return re, im


def smearing(staple, temporal):
    cr, ci = staple
    ur, ui = temporal

    def omega_re(j, k):
        t = cr[j][0] * ur[k][0] + ci[j][0] * ui[k][0]
        for m in (1, 2):
            t = t + (cr[j][m] * ur[k][m] + ci[j][m] * ui[k][m])
        return t

    def omega_im(j, k):
        t = ci[j][0] * ur[k][0] - cr[j][0] * ui[k][0]
        for m in (1, 2):
            t = t + (ci[j][m] * ur[k][m] - cr[j][m] * ui[k][m])
        return t

    half = 0.5 * SMEAR
    diag = [omega_im(j, j) for j in range(3)]
    third = (diag[0] + diag[1] + diag[2]) * (1.0 / 3.0)
    d = [(x - third) * SMEAR for x in diag]
    g = {}
    for j, k in ((0, 1), (0, 2), (1, 2)):
        g[j, k] = (
            (omega_im(j, k) + omega_im(k, j)) * half,
            (omega_re(k, j) - omega_re(j, k)) * half,
        )
    s, s01, s02, s12, q = squared(d, g[0, 1], g[0, 2], g[1, 2])
    p = (s[0] + s[1] + s[2]) * 0.5
    f1 = p * (-1.0 / 6.0) + 1.0
    f0i = q * (-1.0 / 6.0)
    re = [[None] * 3 for _ in range(3)]
    im = [[None] * 3 for _ in range(3)]
    for j in range(3):
        re[j][j] = 1.0 - 0.5 * s[j]
        im[j][j] = f0i + f1 * d[j]
    for j, k, h in ((0, 1, s01), (0, 2, s02), (1, 2, s12)):
        a = f1 * g[j, k][0]
        b = f1 * g[j, k][1]
        c = 0.5 * h[0]
        e = 0.5 * h[1]
        re[j][k], re[k][j] = -b - c, b - c
        im[j][k], im[k][j] = a - e, a + e
    return re, im


def slice_of(rows, n, t):
    return [rows[n, a, pl.ds(t, ROWS, stride=NT_LOCAL), :] for a in range(8)]


def unit():
    one = jnp.ones((ROWS, LANES), jnp.float32)
    zero = jnp.zeros((ROWS, LANES), jnp.float32)
    return (
        [[one if i == j else zero for j in range(3)] for i in range(3)],
        [[zero] * 3 for _ in range(3)],
    )


def plane_terms(spatial, temporal, ahead, above, below):
    forward = forward_term(spatial, mapped(above, temporal), ahead)
    return plus(forward, mapped(below, backward_term(spatial, temporal, ahead)))


def make_links(rows, links):
    def step(t, carry):
        for direction in range(4):
            write(links, link_of(slice_of(rows, direction, t)), direction, t)
        return carry

    lax.fori_loop(0, NT_LOCAL, step, 0)


def make_staple(links, staple):
    def step(t, carry):
        terms = plane_terms(
            read(links, 1, t), read(links, 3, t), read(links, 1, t + 1), from_y_above, from_y_below
        )
        write(staple, terms, t)
        terms = plane_terms(
            read(links, 2, t), read(links, 3, t), read(links, 2, t + 1), from_z_above, from_z_below
        )
        write(staple, plus(read(staple, t), terms), t)
        return carry

    lax.fori_loop(0, NT_LOCAL - 1, step, 0)


def first_kernel(coeffs, coeffs_by_row, first, links, staple, rows, sem):
    copy = pltpu.make_async_copy(coeffs.at[pl.ds(0, 3), :, :, 0, :], first, sem)
    copy.start()
    copy.wait()

    @pl.when(lax.rem(lax.axis_index("tm"), 16) == 0)
    def _():
        fetch = pltpu.make_async_copy(coeffs_by_row, rows, sem)
        fetch.start()
        fetch.wait()
        make_links(rows, links)

    @pl.when(lax.axis_index("tm") == 0)
    def _():
        make_staple(links, staple)


def links_kernel(rows, links_before, links, sent):
    del links_before
    for n, direction in enumerate((0, 3)):
        for a in range(8):
            sent[n, a] = rows[direction, a]

    @pl.when(lax.rem(lax.axis_index("tm"), 16) != 0)
    def _():
        make_links(rows, links)


def staple_kernel(links, staple_before, staple):
    del staple_before

    @pl.when(lax.axis_index("tm") != 0)
    def _():
        make_staple(links, staple)


def chain_steps(high, low, links, staple, rows, other_links, terms, later, put):
    def step(i, carry):
        t = high - 1 - i
        write(other_links, link_of(slice_of(rows, 1, t)), 1)
        write(other_links, link_of(slice_of(rows, 0, t)), 2)
        write(
            terms,
            plus(
                read(staple, t),
                forward_term(read(links, 0, t), read(other_links, 1), read(links, 0, t + 1)),
            ),
        )
        write(
            terms,
            plus(
                read(terms),
                backward_term(read(other_links, 2), read(other_links, 1), read(other_links, 0)),
            ),
        )
        temporal = read(links, 3, t)
        smeared = mul(smearing(read(terms), temporal), temporal)
        running = mul(smeared, read(later))
        write(later, running)
        put(t, running)
        write(other_links, read(other_links, 2), 0)
        return carry

    lax.fori_loop(0, high - low, step, 0)


def late_chain_kernel(links, staple, rows, partial, other_last, other_links, terms, later):
    last = NT_LOCAL - 1
    for n in range(2):
        write(other_last, link_of(slice_of(rows, n, last)), n)

    def put(t, product):
        write(partial, product, t - SPLIT)

    @pl.when(lax.axis_index("tm") != 0)
    def _():
        write(other_links, read(other_last, 0), 0)
        write(later, unit())
        chain_steps(last, SPLIT, links, staple, rows, other_links, terms, later, put)


def early_chain_kernel(
    links, staple, rows, late, other_last, next_rows, partial, last_terms, other_links, terms, later, ahead
):
    def put(t, product):
        write(partial, product, t)

    @pl.when(lax.axis_index("tm") != 0)
    def _():
        write(other_links, link_of(slice_of(rows, 0, SPLIT)), 0)
        write(later, read(late, 0))
        chain_steps(SPLIT, 0, links, staple, rows, other_links, terms, later, put)

    last = NT_LOCAL - 1
    for direction in range(3):
        write(ahead, link_of([next_rows[direction, a] for a in range(8)]), direction)
    temporal = read(links, 3, last)
    write(
        last_terms,
        plane_terms(read(links, 1, last), temporal, read(ahead, 1), from_y_above, from_y_below),
    )
    for term in (
        lambda: plane_terms(read(links, 2, last), temporal, read(ahead, 2), from_z_above, from_z_below),
        lambda: forward_term(read(links, 0, last), read(other_last, 1), read(ahead, 0)),
    ):
        write(last_terms, plus(read(last_terms), term()))


def first_slab_kernel(
    links, staple, rows, other_last, late_before, early_before, late, early, other_links, terms, later
):
    del late_before, early_before

    def put_late(t, product):
        write(late, product, t - SPLIT)

    def put_early(t, product):
        write(early, product, t)

    @pl.when(lax.axis_index("tm") == 0)
    def _():
        write(other_links, read(other_last, 0), 0)
        write(later, unit())
        last = NT_LOCAL - 1
        chain_steps(last, SPLIT, links, staple, rows, other_links, terms, later, put_late)
        chain_steps(SPLIT, 0, links, staple, rows, other_links, terms, later, put_early)


def pick_kernel(ahead, after, out):
    del after
    out[...] = ahead[0]


def last_slice_kernel(links, other_last, last_terms, other_next, partial, smeared_last, total, ahead):
    write(ahead, link_of([other_next[a] for a in range(8)]))
    temporal = read(links, 3, NT_LOCAL - 1)
    terms = plus(
        read(last_terms), backward_term(read(other_last, 0), read(other_last, 1), read(ahead))
    )
    write(ahead, terms)
    smeared = mul(smearing(read(ahead), temporal), temporal)
    write(smeared_last, smeared)
    write(total, mul(read(partial, 0), read(smeared_last)))


def suffixes(low, peers, own, by1, by2, by3, held):
    digit = lax.rem(lax.axis_index("tm") // low, 4)
    for k, ref in zip((0, *peers), (own, by1, by2, by3)):
        for a in range(18):
            held[k, a] = ref[a]
    third = read(held, 3 ^ digit)
    second = mul(read(held, 2 ^ digit), third)
    first = mul(read(held, 1 ^ digit), second)
    zeroth = read(held, digit)
    for k, matrix in enumerate((first, second, third, unit())):
        write(held, matrix, 4 + k)
    return zeroth, 4 + digit


def level_kernel(low, own, by1, by2, by3, new_total, suffix, held):
    zeroth, at = suffixes(low, PEERS, own, by1, by2, by3, held)
    write(new_total, mul(zeroth, read(held, 4)))
    write(suffix, read(held, at))


def tail_kernel(tail, suffix, new_tail):
    write(new_tail, mul(read(tail), read(suffix)))


def closing_kernel(low, own, by1, by2, by3, tail, early, late, out, held, rows, sems):
    _, at = suffixes(low, LAST_PEERS, own, by1, by2, by3, held)
    write(held, mul(read(tail), read(held, at)), 0)
    last = NT_LOCAL - 1
    copies = []
    for i in range(3):

        def put(t, row, i=i):
            for part in range(2):
                for j in range(3):
                    rows[9 * part + 3 * i + j, pl.ds(t, ROWS, stride=NT_LOCAL), :] = row[part][j]

        for partial, low, high in ((early, 0, SPLIT), (late, SPLIT, last)):

            for t in range(low, high):
                left = [[partial[t - low, 9 * part + 3 * i + j] for j in range(3)] for part in range(2)]
                put(t, row_times(left, read(held, 0)))
        put(last, [[held[0, 9 * part + 3 * i + j] for j in range(3)] for part in range(2)])
        for part in range(2):
            planes = pl.ds(9 * part + 3 * i, 3)
            copies.append(pltpu.make_async_copy(rows.at[planes], out.at[planes], sems.at[i, part]))
            copies[-1].start()
    for copy in copies:
        copy.wait()


def params():
    return pltpu.CompilerParams(vmem_limit_bytes=VMEM_LIMIT)


def field(*lead):
    return jax.ShapeDtypeStruct((*lead, 18, ROWS, LANES), jnp.float32)


def cost(flops):
    return pl.CostEstimate(flops=flops, bytes_accessed=1_000_000, transcendentals=0)


def block(*shape):
    return jax.ShapeDtypeStruct(shape, jnp.float32)


def shards(coeffs):
    count = lax.axis_size("tm")
    coeffs = coeffs.reshape(4, 8, NT_LOCAL, ROWS, LANES).swapaxes(2, 3)
    rows = coeffs.reshape(4, 8, ROWS * NT_LOCAL, LANES)
    first, links, staple = pl.pallas_call(
        first_kernel,
        out_shape=(block(3, 8, ROWS, LANES), field(4, NT_LOCAL), field(NT_LOCAL)),
        in_specs=[pl.BlockSpec(memory_space=pltpu.HBM)] * 2,
        out_specs=(WHOLE, WHOLE, WHOLE),
        scratch_shapes=[
            pltpu.VMEM((4, 8, ROWS * NT_LOCAL, LANES), jnp.float32),
            pltpu.SemaphoreType.DMA,
        ],
        compiler_params=params(),
        cost_estimate=cost(1_000_000_000),
        name="first_slice",
    )(
        pltpu.with_memory_space_constraint(coeffs, pltpu.HBM),
        pltpu.with_memory_space_constraint(rows, pltpu.HBM),
    )
    ahead = lax.ppermute(first, "tm", [((i + 1) % count, i) for i in range(count)])
    links, sent = pl.pallas_call(
        links_kernel,
        out_shape=(field(4, NT_LOCAL), block(2, 8, ROWS * NT_LOCAL, LANES)),
        in_specs=[WHOLE] * 2,
        out_specs=(WHOLE, WHOLE),
        input_output_aliases={1: 0},
        compiler_params=params(),
        cost_estimate=cost(10_000_000),
        name="links",
    )(rows, links)
    other_rows = lax.ppermute(sent, "space", [(0, 1), (1, 0)])
    staple = pl.pallas_call(
        staple_kernel,
        out_shape=field(NT_LOCAL),
        in_specs=[WHOLE] * 2,
        out_specs=WHOLE,
        input_output_aliases={1: 0},
        compiler_params=params(),
        cost_estimate=cost(20_000_000_000),
        name="staple",
    )(links, staple)
    chain_scratch = [
        pltpu.VMEM((3, 18, ROWS, LANES), jnp.float32),
        pltpu.VMEM((18, ROWS, LANES), jnp.float32),
        pltpu.VMEM((18, ROWS, LANES), jnp.float32),
    ]
    late, other_last = pl.pallas_call(
        late_chain_kernel,
        out_shape=(field(NT_LOCAL - 1 - SPLIT), field(2)),
        in_specs=[WHOLE] * 3,
        out_specs=(WHOLE, WHOLE),
        scratch_shapes=chain_scratch,
        compiler_params=params(),
        cost_estimate=cost(8_000_000),
        name="late_chain",
    )(links, staple, other_rows)
    ahead_x = pl.pallas_call(
        pick_kernel,
        out_shape=block(8, ROWS, LANES),
        in_specs=[WHOLE, WHOLE],
        out_specs=WHOLE,
        compiler_params=params(),
        name="pick",
    )(ahead, late)
    other_ahead = lax.ppermute(ahead_x, "space", [(0, 1), (1, 0)])
    early, last_terms = pl.pallas_call(
        early_chain_kernel,
        out_shape=(field(SPLIT), field()),
        in_specs=[WHOLE] * 6,
        out_specs=(WHOLE, WHOLE),
        scratch_shapes=chain_scratch + [pltpu.VMEM((3, 18, ROWS, LANES), jnp.float32)],
        compiler_params=params(),
        cost_estimate=cost(8_000_000),
        name="early_chain",
    )(links, staple, other_rows, late, other_last, ahead)
    tail, total = pl.pallas_call(
        last_slice_kernel,
        out_shape=(field(), field()),
        in_specs=[WHOLE] * 5,
        out_specs=(WHOLE, WHOLE),
        scratch_shapes=[pltpu.VMEM((18, ROWS, LANES), jnp.float32)],
        compiler_params=params(),
        cost_estimate=cost(3_000_000),
        name="last_slice",
    )(links, other_last, last_terms, other_ahead, early)
    late, early = pl.pallas_call(
        first_slab_kernel,
        out_shape=(field(NT_LOCAL - 1 - SPLIT), field(SPLIT)),
        in_specs=[WHOLE] * 6,
        out_specs=(WHOLE, WHOLE),
        input_output_aliases={4: 0, 5: 1},
        scratch_shapes=chain_scratch,
        compiler_params=params(),
        name="first_slab",
    )(links, staple, other_rows, other_last, late, early)
    low = 1
    while True:
        peers = LAST_PEERS if low * 4 >= count else PEERS
        received = [
            lax.ppermute(total, "tm", [(i, i ^ (low * k)) for i in range(count)]) for k in peers
        ]
        held = pltpu.VMEM((8, 18, ROWS, LANES), jnp.float32)
        if low * 4 >= count:
            break

        def level(*refs, low=low):
            level_kernel(low, *refs)

        total, suffix = pl.pallas_call(
            level,
            out_shape=(field(), field()),
            in_specs=[WHOLE] * 4,
            out_specs=(WHOLE, WHOLE),
            scratch_shapes=[held],
            compiler_params=params(),
            name=f"level_{low}",
        )(total, *received)
        tail = pl.pallas_call(
            tail_kernel,
            out_shape=field(),
            in_specs=[WHOLE] * 2,
            out_specs=WHOLE,
            compiler_params=params(),
            name=f"tail_{low}",
        )(tail, suffix)
        low *= 4

    def closing(*refs, low=low):
        closing_kernel(low, *refs)

    out = pl.pallas_call(
        closing,
        out_shape=block(18, ROWS * NT_LOCAL, LANES),
        in_specs=[WHOLE] * 7,
        out_specs=pl.BlockSpec(memory_space=pltpu.HBM),
        scratch_shapes=[
            held,
            pltpu.VMEM((18, ROWS * NT_LOCAL, LANES), jnp.float32),
            pltpu.SemaphoreType.DMA((3, 2)),
        ],
        compiler_params=params(),
        name="closing",
    )(total, *received, tail, early, late)
    out = out.reshape(18, ROWS, NT_LOCAL, LANES).swapaxes(1, 2)
    return out.reshape(2, 3, 3, 1, NT_LOCAL, ROWS * LANES)


def solution(mesh):
    in_specs = (P(None, None, "space", "tm", None),)
    out_specs = P(None, None, None, "space", "tm", None)
    return jax.shard_map(shards, mesh=mesh, in_specs=in_specs, out_specs=out_specs, check_vma=False)
```

```python
import jax
import jax.numpy as jnp
from jax import lax
from jax.experimental import pallas as pl
from jax.experimental.pallas import tpu as pltpu
from jax.sharding import PartitionSpec as P

ZDIM = 32
LANES = 128
ROWS = 8
NT_LOCAL = 8
SMEAR = 0.1
SPLIT = 1
PEERS = (1, 3, 2)
LAST_PEERS = (1, 3, 2)
ROOT_THIRD = 1.0 / 3.0**0.5
VMEM_LIMIT = 48 * 1024 * 1024
WHOLE = pl.BlockSpec(memory_space=pltpu.VMEM)


def read(ref, *index):
    re = [[ref[(*index, 3 * i + j)] for j in range(3)] for i in range(3)]
    im = [[ref[(*index, 9 + 3 * i + j)] for j in range(3)] for i in range(3)]
    return re, im


def write(ref, matrix, *index):
    for part in range(2):
        for i in range(3):
            for j in range(3):
                ref[(*index, 9 * part + 3 * i + j)] = matrix[part][i][j]


def row_times(row, matrix, conj_left=False, conj_right=False):
    a, b = row
    c, d = matrix
    out_re, out_im = [], []
    for j in range(3):
        rr = a[0] * c[0][j]
        ii = b[0] * d[0][j]
        ri = a[0] * d[0][j]
        ir = b[0] * c[0][j]
        for m in (1, 2):
            rr = rr + a[m] * c[m][j]
            ii = ii + b[m] * d[m][j]
            ri = ri + a[m] * d[m][j]
            ir = ir + b[m] * c[m][j]
        out_re.append(rr + ii if conj_left != conj_right else rr - ii)
        if conj_left and conj_right:
            out_im.append(-(ri + ir))
        elif conj_left:
            out_im.append(ri - ir)
        elif conj_right:
            out_im.append(ir - ri)
        else:
            out_im.append(ri + ir)
    return out_re, out_im


def mul(left, right):
    re, im = [], []
    for i in range(3):
        r, m = row_times((left[0][i], left[1][i]), right)
        re.append(r)
        im.append(m)
    return re, im


def transposed(matrix):
    return tuple([[part[j][i] for j in range(3)] for i in range(3)] for part in matrix)


def forward_term(link, temporal, ahead):
    turned = transposed(ahead)
    re, im = [], []
    for i in range(3):
        row = row_times((link[0][i], link[1][i]), temporal)
        r, m = row_times(row, turned, conj_right=True)
        re.append(r)
        im.append(m)
    return re, im


def backward_term(link, temporal, ahead):
    turned = transposed(link)
    re, im = [], []
    for i in range(3):
        row = row_times((turned[0][i], turned[1][i]), temporal, conj_left=True)
        r, m = row_times(row, ahead)
        re.append(r)
        im.append(m)
    return re, im


def plus(left, right):
    return tuple(
        [[left[p][i][j] + right[p][i][j] for j in range(3)] for i in range(3)] for p in range(2)
    )


def mapped(f, matrix):
    return tuple([[f(part[i][j]) for j in range(3)] for i in range(3)] for part in matrix)


def lane():
    return lax.broadcasted_iota(jnp.int32, (ROWS, LANES), 1)


def from_y_above(x):
    r = pltpu.roll(x, LANES - ZDIM, 1)
    return jnp.where(lane() >= LANES - ZDIM, pltpu.roll(r, ROWS - 1, 0), r)


def from_y_below(x):
    r = pltpu.roll(x, ZDIM, 1)
    return jnp.where(lane() < ZDIM, pltpu.roll(r, 1, 0), r)


def from_z_above(x):
    edge = lane() % ZDIM == ZDIM - 1
    return jnp.where(edge, pltpu.roll(x, ZDIM - 1, 1), pltpu.roll(x, LANES - 1, 1))


def from_z_below(x):
    edge = lane() % ZDIM == 0
    return jnp.where(edge, pltpu.roll(x, LANES - ZDIM + 1, 1), pltpu.roll(x, 1, 1))


def squared(d, g01, g02, g12):
    n01 = g01[0] * g01[0] + g01[1] * g01[1]
    n02 = g02[0] * g02[0] + g02[1] * g02[1]
    n12 = g12[0] * g12[0] + g12[1] * g12[1]
    s = (d[0] * d[0] + (n01 + n02), d[1] * d[1] + (n01 + n12), d[2] * d[2] + (n02 + n12))
    k = (g01[0] * g12[0] - g01[1] * g12[1], g01[0] * g12[1] + g01[1] * g12[0])
    s02 = (k[0] - d[1] * g02[0], k[1] - d[1] * g02[1])
    s01 = (
        (g02[0] * g12[0] + g02[1] * g12[1]) - d[2] * g01[0],
        (g02[1] * g12[0] - g02[0] * g12[1]) - d[2] * g01[1],
    )
    s12 = (
        (g01[0] * g02[0] + g01[1] * g02[1]) - d[0] * g12[0],
        (g01[0] * g02[1] - g01[1] * g02[0]) - d[0] * g12[1],
    )
    det = (
        d[0] * (d[1] * d[2] - n12)
        - d[1] * n02
        - d[2] * n01
        + 2.0 * (k[0] * g02[0] + k[1] * g02[1])
    )
    return s, s01, s02, s12, det


def link_of(c):
    d2 = c[7] * (-2.0 * ROOT_THIRD)
    e = c[7] * ROOT_THIRD
    d = (e + c[2], e - c[2], d2)
    g01, g02, g12 = (c[0], -c[1]), (c[3], -c[4]), (c[5], -c[6])
    s, s01, s02, s12, det = squared(d, g01, g02, g12)
    p = (s[0] + s[1] + s[2]) * 0.125
    q = det * 0.125
    qq = q * q
    w = (p * (-1.0 / 5040.0) + 1.0 / 120.0) * p - 1.0 / 6.0
    f0r = qq * (p * (1.0 / 20160.0) - 1.0 / 720.0) + 1.0
    f0i = q * w
    f1r = q * ((p * (0.5 / 13440.0) - 0.5 / 360.0) * p + 0.5 / 24.0)
    f1i = (p * w + qq * (-1.0 / 5040.0)) * 0.5 + 0.5
    f2r = ((p * (0.25 / 40320.0) - 0.25 / 720.0) * p + 0.25 / 24.0) * p + (qq * (0.25 / 40320.0) - 0.125)
    f2i = q * (p * (-0.5 / 5040.0) + 0.25 / 120.0)
    re = [[None] * 3 for _ in range(3)]
    im = [[None] * 3 for _ in range(3)]
    for j in range(3):
        re[j][j] = f0r + (f1r * d[j] + f2r * s[j])
        im[j][j] = f0i + (f1i * d[j] + f2i * s[j])
    for j, k, g, h in ((0, 1, g01, s01), (0, 2, g02, s02), (1, 2, g12, s12)):
        rr = f1r * g[0] + f2r * h[0]
        ii = f1i * g[1] + f2i * h[1]
        ir = f1i * g[0] + f2i * h[0]
        ri = f1r * g[1] + f2r * h[1]
        re[j][k], re[k][j] = rr - ii, rr + ii
        im[j][k], im[k][j] = ir + ri, ir - ri
    return re, im


def smearing(staple, temporal):
    cr, ci = staple
    ur, ui = temporal

    def omega_re(j, k):
        t = cr[j][0] * ur[k][0] + ci[j][0] * ui[k][0]
        for m in (1, 2):
            t = t + (cr[j][m] * ur[k][m] + ci[j][m] * ui[k][m])
        return t

    def omega_im(j, k):
        t = ci[j][0] * ur[k][0] - cr[j][0] * ui[k][0]
        for m in (1, 2):
            t = t + (ci[j][m] * ur[k][m] - cr[j][m] * ui[k][m])
        return t

    half = 0.5 * SMEAR
    diag = [omega_im(j, j) for j in range(3)]
    third = (diag[0] + diag[1] + diag[2]) * (1.0 / 3.0)
    d = [(x - third) * SMEAR for x in diag]
    g = {}
    for j, k in ((0, 1), (0, 2), (1, 2)):
        g[j, k] = (
            (omega_im(j, k) + omega_im(k, j)) * half,
            (omega_re(k, j) - omega_re(j, k)) * half,
        )
    s, s01, s02, s12, q = squared(d, g[0, 1], g[0, 2], g[1, 2])
    p = (s[0] + s[1] + s[2]) * 0.5
    f1 = p * (-1.0 / 6.0) + 1.0
    f0i = q * (-1.0 / 6.0)
    re = [[None] * 3 for _ in range(3)]
    im = [[None] * 3 for _ in range(3)]
    for j in range(3):
        re[j][j] = 1.0 - 0.5 * s[j]
        im[j][j] = f0i + f1 * d[j]
    for j, k, h in ((0, 1, s01), (0, 2, s02), (1, 2, s12)):
        a = f1 * g[j, k][0]
        b = f1 * g[j, k][1]
        c = 0.5 * h[0]
        e = 0.5 * h[1]
        re[j][k], re[k][j] = -b - c, b - c
        im[j][k], im[k][j] = a - e, a + e
    return re, im


def slice_of(rows, n, t):
    return [rows[n, a, pl.ds(t, ROWS, stride=NT_LOCAL), :] for a in range(8)]


def unit():
    one = jnp.ones((ROWS, LANES), jnp.float32)
    zero = jnp.zeros((ROWS, LANES), jnp.float32)
    return (
        [[one if i == j else zero for j in range(3)] for i in range(3)],
        [[zero] * 3 for _ in range(3)],
    )


def plane_terms(spatial, temporal, ahead, above, below):
    forward = forward_term(spatial, mapped(above, temporal), ahead)
    return plus(forward, mapped(below, backward_term(spatial, temporal, ahead)))


def make_links(rows, links):
    def step(t, carry):
        for direction in range(4):
            write(links, link_of(slice_of(rows, direction, t)), direction, t)
        return carry

    lax.fori_loop(0, NT_LOCAL, step, 0)


def make_staple(links, staple):
    def step(t, carry):
        terms = plane_terms(
            read(links, 1, t), read(links, 3, t), read(links, 1, t + 1), from_y_above, from_y_below
        )
        write(staple, terms, t)
        terms = plane_terms(
            read(links, 2, t), read(links, 3, t), read(links, 2, t + 1), from_z_above, from_z_below
        )
        write(staple, plus(read(staple, t), terms), t)
        return carry

    lax.fori_loop(0, NT_LOCAL - 1, step, 0)


def first_kernel(coeffs, coeffs_by_row, first, links, staple, rows, sem):
    copy = pltpu.make_async_copy(coeffs.at[pl.ds(0, 3), :, :, 0, :], first, sem)
    copy.start()
    copy.wait()

    @pl.when(lax.rem(lax.axis_index("tm"), 16) == 0)
    def _():
        fetch = pltpu.make_async_copy(coeffs_by_row, rows, sem)
        fetch.start()
        fetch.wait()
        make_links(rows, links)

    @pl.when(lax.axis_index("tm") == 0)
    def _():
        make_staple(links, staple)


def links_kernel(rows, links_before, links, sent):
    del links_before
    for n, direction in enumerate((0, 3)):
        for a in range(8):
            sent[n, a] = rows[direction, a]

    @pl.when(lax.rem(lax.axis_index("tm"), 16) != 0)
    def _():
        make_links(rows, links)


def staple_kernel(links, staple_before, staple):
    del staple_before

    @pl.when(lax.axis_index("tm") != 0)
    def _():
        make_staple(links, staple)


def chain_steps(high, low, links, staple, rows, other_links, terms, later, put):
    def step(i, carry):
        t = high - 1 - i
        write(other_links, link_of(slice_of(rows, 1, t)), 1)
        write(other_links, link_of(slice_of(rows, 0, t)), 2)
        write(
            terms,
            plus(
                read(staple, t),
                forward_term(read(links, 0, t), read(other_links, 1), read(links, 0, t + 1)),
            ),
        )
        write(
            terms,
            plus(
                read(terms),
                backward_term(read(other_links, 2), read(other_links, 1), read(other_links, 0)),
            ),
        )
        temporal = read(links, 3, t)
        smeared = mul(smearing(read(terms), temporal), temporal)
        running = mul(smeared, read(later))
        write(later, running)
        put(t, running)
        write(other_links, read(other_links, 2), 0)
        return carry

    lax.fori_loop(0, high - low, step, 0)


def late_chain_kernel(links, staple, rows, partial, other_last, other_links, terms, later):
    last = NT_LOCAL - 1
    for n in range(2):
        write(other_last, link_of(slice_of(rows, n, last)), n)
    write(other_links, read(other_last, 0), 0)
    write(later, unit())

    def put(t, product):
        write(partial, product, t - SPLIT)

    chain_steps(last, SPLIT, links, staple, rows, other_links, terms, later, put)


def early_chain_kernel(
    links, staple, rows, late, other_last, next_rows, partial, last_terms, other_links, terms, later, ahead
):
    write(other_links, link_of(slice_of(rows, 0, SPLIT)), 0)
    write(later, read(late, 0))

    def put(t, product):
        write(partial, product, t)

    chain_steps(SPLIT, 0, links, staple, rows, other_links, terms, later, put)
    last = NT_LOCAL - 1
    for direction in range(3):
        write(ahead, link_of([next_rows[direction, a] for a in range(8)]), direction)
    temporal = read(links, 3, last)
    write(
        last_terms,
        plane_terms(read(links, 1, last), temporal, read(ahead, 1), from_y_above, from_y_below),
    )
    for term in (
        lambda: plane_terms(read(links, 2, last), temporal, read(ahead, 2), from_z_above, from_z_below),
        lambda: forward_term(read(links, 0, last), read(other_last, 1), read(ahead, 0)),
    ):
        write(last_terms, plus(read(last_terms), term()))


def pick_kernel(ahead, after, out):
    del after
    out[...] = ahead[0]


def last_slice_kernel(links, other_last, last_terms, other_next, partial, smeared_last, total, ahead):
    write(ahead, link_of([other_next[a] for a in range(8)]))
    temporal = read(links, 3, NT_LOCAL - 1)
    terms = plus(
        read(last_terms), backward_term(read(other_last, 0), read(other_last, 1), read(ahead))
    )
    write(ahead, terms)
    smeared = mul(smearing(read(ahead), temporal), temporal)
    write(smeared_last, smeared)
    write(total, mul(read(partial, 0), read(smeared_last)))


def suffixes(low, peers, own, by1, by2, by3, held):
    digit = lax.rem(lax.axis_index("tm") // low, 4)
    for k, ref in zip((0, *peers), (own, by1, by2, by3)):
        for a in range(18):
            held[k, a] = ref[a]
    third = read(held, 3 ^ digit)
    second = mul(read(held, 2 ^ digit), third)
    first = mul(read(held, 1 ^ digit), second)
    zeroth = read(held, digit)
    for k, matrix in enumerate((first, second, third, unit())):
        write(held, matrix, 4 + k)
    return zeroth, 4 + digit


def level_kernel(low, own, by1, by2, by3, new_total, suffix, held):
    zeroth, at = suffixes(low, PEERS, own, by1, by2, by3, held)
    write(new_total, mul(zeroth, read(held, 4)))
    write(suffix, read(held, at))


def tail_kernel(tail, suffix, new_tail):
    write(new_tail, mul(read(tail), read(suffix)))


def closing_kernel(low, own, by1, by2, by3, tail, early, late, out, held, rows, sems):
    _, at = suffixes(low, LAST_PEERS, own, by1, by2, by3, held)
    write(held, mul(read(tail), read(held, at)), 0)
    last = NT_LOCAL - 1
    copies = []
    for i in range(3):

        def put(t, row, i=i):
            for part in range(2):
                for j in range(3):
                    rows[9 * part + 3 * i + j, pl.ds(t, ROWS, stride=NT_LOCAL), :] = row[part][j]

        for partial, low, high in ((early, 0, SPLIT), (late, SPLIT, last)):

            for t in range(low, high):
                left = [[partial[t - low, 9 * part + 3 * i + j] for j in range(3)] for part in range(2)]
                put(t, row_times(left, read(held, 0)))
        put(last, [[held[0, 9 * part + 3 * i + j] for j in range(3)] for part in range(2)])
        for part in range(2):
            planes = pl.ds(9 * part + 3 * i, 3)
            copies.append(pltpu.make_async_copy(rows.at[planes], out.at[planes], sems.at[i, part]))
            copies[-1].start()
    for copy in copies:
        copy.wait()


def params():
    return pltpu.CompilerParams(vmem_limit_bytes=VMEM_LIMIT)


def field(*lead):
    return jax.ShapeDtypeStruct((*lead, 18, ROWS, LANES), jnp.float32)


def cost(flops):
    return pl.CostEstimate(flops=flops, bytes_accessed=1_000_000, transcendentals=0)


def block(*shape):
    return jax.ShapeDtypeStruct(shape, jnp.float32)


def shards(coeffs):
    count = lax.axis_size("tm")
    coeffs = coeffs.reshape(4, 8, NT_LOCAL, ROWS, LANES).swapaxes(2, 3)
    rows = coeffs.reshape(4, 8, ROWS * NT_LOCAL, LANES)
    first, links, staple = pl.pallas_call(
        first_kernel,
        out_shape=(block(3, 8, ROWS, LANES), field(4, NT_LOCAL), field(NT_LOCAL)),
        in_specs=[pl.BlockSpec(memory_space=pltpu.HBM)] * 2,
        out_specs=(WHOLE, WHOLE, WHOLE),
        scratch_shapes=[
            pltpu.VMEM((4, 8, ROWS * NT_LOCAL, LANES), jnp.float32),
            pltpu.SemaphoreType.DMA,
        ],
        compiler_params=params(),
        cost_estimate=cost(1_000_000_000),
        name="first_slice",
    )(
        pltpu.with_memory_space_constraint(coeffs, pltpu.HBM),
        pltpu.with_memory_space_constraint(rows, pltpu.HBM),
    )
    ahead = lax.ppermute(first, "tm", [((i + 1) % count, i) for i in range(count)])
    links, sent = pl.pallas_call(
        links_kernel,
        out_shape=(field(4, NT_LOCAL), block(2, 8, ROWS * NT_LOCAL, LANES)),
        in_specs=[WHOLE] * 2,
        out_specs=(WHOLE, WHOLE),
        input_output_aliases={1: 0},
        compiler_params=params(),
        cost_estimate=cost(10_000_000),
        name="links",
    )(rows, links)
    other_rows = lax.ppermute(sent, "space", [(0, 1), (1, 0)])
    staple = pl.pallas_call(
        staple_kernel,
        out_shape=field(NT_LOCAL),
        in_specs=[WHOLE] * 2,
        out_specs=WHOLE,
        input_output_aliases={1: 0},
        compiler_params=params(),
        cost_estimate=cost(20_000_000_000),
        name="staple",
    )(links, staple)
    chain_scratch = [
        pltpu.VMEM((3, 18, ROWS, LANES), jnp.float32),
        pltpu.VMEM((18, ROWS, LANES), jnp.float32),
        pltpu.VMEM((18, ROWS, LANES), jnp.float32),
    ]
    late, other_last = pl.pallas_call(
        late_chain_kernel,
        out_shape=(field(NT_LOCAL - 1 - SPLIT), field(2)),
        in_specs=[WHOLE] * 3,
        out_specs=(WHOLE, WHOLE),
        scratch_shapes=chain_scratch,
        compiler_params=params(),
        cost_estimate=cost(8_000_000),
        name="late_chain",
    )(links, staple, other_rows)
    ahead_x = pl.pallas_call(
        pick_kernel,
        out_shape=block(8, ROWS, LANES),
        in_specs=[WHOLE, WHOLE],
        out_specs=WHOLE,
        compiler_params=params(),
        name="pick",
    )(ahead, late)
    other_ahead = lax.ppermute(ahead_x, "space", [(0, 1), (1, 0)])
    early, last_terms = pl.pallas_call(
        early_chain_kernel,
        out_shape=(field(SPLIT), field()),
        in_specs=[WHOLE] * 6,
        out_specs=(WHOLE, WHOLE),
        scratch_shapes=chain_scratch + [pltpu.VMEM((3, 18, ROWS, LANES), jnp.float32)],
        compiler_params=params(),
        cost_estimate=cost(8_000_000),
        name="early_chain",
    )(links, staple, other_rows, late, other_last, ahead)
    tail, total = pl.pallas_call(
        last_slice_kernel,
        out_shape=(field(), field()),
        in_specs=[WHOLE] * 5,
        out_specs=(WHOLE, WHOLE),
        scratch_shapes=[pltpu.VMEM((18, ROWS, LANES), jnp.float32)],
        compiler_params=params(),
        cost_estimate=cost(3_000_000),
        name="last_slice",
    )(links, other_last, last_terms, other_ahead, early)
    low = 1
    while True:
        peers = LAST_PEERS if low * 4 >= count else PEERS
        received = [
            lax.ppermute(total, "tm", [(i, i ^ (low * k)) for i in range(count)]) for k in peers
        ]
        held = pltpu.VMEM((8, 18, ROWS, LANES), jnp.float32)
        if low * 4 >= count:
            break

        def level(*refs, low=low):
            level_kernel(low, *refs)

        total, suffix = pl.pallas_call(
            level,
            out_shape=(field(), field()),
            in_specs=[WHOLE] * 4,
            out_specs=(WHOLE, WHOLE),
            scratch_shapes=[held],
            compiler_params=params(),
            name=f"level_{low}",
        )(total, *received)
        tail = pl.pallas_call(
            tail_kernel,
            out_shape=field(),
            in_specs=[WHOLE] * 2,
            out_specs=WHOLE,
            compiler_params=params(),
            name=f"tail_{low}",
        )(tail, suffix)
        low *= 4

    def closing(*refs, low=low):
        closing_kernel(low, *refs)

    out = pl.pallas_call(
        closing,
        out_shape=block(18, ROWS * NT_LOCAL, LANES),
        in_specs=[WHOLE] * 7,
        out_specs=pl.BlockSpec(memory_space=pltpu.HBM),
        scratch_shapes=[
            held,
            pltpu.VMEM((18, ROWS * NT_LOCAL, LANES), jnp.float32),
            pltpu.SemaphoreType.DMA((3, 2)),
        ],
        compiler_params=params(),
        name="closing",
    )(total, *received, tail, early, late)
    out = out.reshape(18, ROWS, NT_LOCAL, LANES).swapaxes(1, 2)
    return out.reshape(2, 3, 3, 1, NT_LOCAL, ROWS * LANES)


def solution(mesh):
    in_specs = (P(None, None, "space", "tm", None),)
    out_specs = P(None, None, None, "space", "tm", None)
    return jax.shard_map(shards, mesh=mesh, in_specs=in_specs, out_specs=out_specs, check_vma=False)
```
